128 devices in a mesh: dp: 64 (over z, y, x_lo, core), tensor: 2 (over x_hi).
Axes of the slice: x: 4 (x_hi: 2, x_lo: 2; x = x_hi * 2 + x_lo), y: 4, z: 4, core: 2. Of those that a mesh axis runs over, the one named last changes fastest.
Arguments:
- activations: bfloat16 [65536, 4096], P(('dp', 'tensor')), may hold values from -6 to 6
- key_grad: bfloat16 [65536, 1024], P('dp', 'tensor'), may hold values from -0.5 to 0.5
- key_weight: bfloat16 [4096, 1024], P(None, 'tensor'), may hold values from -3 to 3
- error_prev: bfloat16 [262144, 1024], P('dp', 'tensor'), may hold values from -6 to 6
- right_prev: float32 [1024, 64], P('tensor'), may hold values from -0.25 to 0.25
Outputs:
- input_grad: bfloat16 [65536, 4096], P(('dp', 'tensor'))
- right_new: float32 [1024, 64], P('tensor')
- error_new: bfloat16 [262144, 1024], P('dp', 'tensor')
The draws below stay inside these ranges and needn't reach their ends.
All inputs are finite; a program needn't handle non-finite values.
Results may differ from the reference program's by a relative error of at most 0.01.
Values may be sent and summed in bfloat16 or wider, within the bound.
A program may use at most 128 MiB of HBM per device.

```python
import jax
import jax.numpy as jnp
from jax import lax

D = 4096
RANK = 64
TOK_DEV = 1024
KV = 1024
TOKENS = 65536
N_DP = 64
N_TENSOR = 2


def steps_of(rng, extent, cuts, low, largest):
    def one(dim, blocks):
        draws = jax.random.uniform(jax.random.fold_in(jax.random.fold_in(rng, 6), dim), (blocks,), jnp.float32, low / len(cuts), largest / len(cuts))
        return jnp.repeat(jnp.exp(draws), extent[dim] // blocks).reshape((-1,) + (1,) * (len(extent) - dim - 1))

    level = one(*cuts[0])
    for cut in cuts[1:]:
        level = level * one(*cut)
    return level


def gaussian(rng, dims, deviation, most, cuts=(), kind=jnp.bfloat16):
    factor_of = steps_of(rng, dims, cuts, -0.22, 0.18) if cuts else 1.0
    values = jax.random.normal(rng, dims, jnp.float32) * deviation * factor_of
    return jnp.minimum(jnp.maximum(values, -most), most).astype(kind)


def setup_inputs(seed: int = 0) -> dict:
    seeds = jax.random.split(jax.random.key(seed), 6)
    return {
        "activations": gaussian(seeds[0], (TOKENS, D), 1.0, 6.0, ((0, 128),)),
        "key_grad": gaussian(seeds[1], (TOKENS, KV), 0.0625, 0.5, ((0, 64), (1, 2))),
        "key_weight": gaussian(seeds[2], (D, KV), 0.5, 3.0, ((1, 2),)),
        "error_prev": gaussian(seeds[3], (N_DP * D, KV), 1.0, 6.0, ((0, 64), (1, 2))),
        "right_prev": gaussian(seeds[4], (KV, RANK), (KV // N_TENSOR) ** -0.5, 0.25, ((0, 2),), jnp.float32),
    }


highest_mode = lax.Precision.HIGHEST

def orthonormal_cols(left_part):
    gram_matrix = jnp.dot(left_part.T, left_part, precision=highest_mode)
    factor_low = jnp.linalg.cholesky(gram_matrix)
    return jax.scipy.linalg.solve_triangular(factor_low, left_part.T, lower=True).T

def reference(activations, key_grad, key_weight, error_prev, right_prev):
    head_block = KV // N_TENSOR
    grouped_acts = activations.reshape(N_DP, TOK_DEV, D)
    grouped_grads = key_grad.reshape(N_DP, TOK_DEV, KV)
    grouped_error = error_prev.reshape(N_DP, D, KV)

    def one_group(inputs):
        acts_group, grads_group, error_group = inputs
        weight_grad = jnp.dot(acts_group.T.astype(jnp.float32), grads_group.astype(jnp.float32), preferred_element_type=jnp.float32)
        return weight_grad + error_group.astype(jnp.float32)
    merged = lax.map(one_group, (grouped_acts, grouped_grads, grouped_error))
    merged = merged.reshape(N_DP, D, N_TENSOR, head_block)
    right_blocks = right_prev.reshape(N_TENSOR, head_block, RANK)
    left_total = jnp.einsum('adtk,tkr->tdr', merged, right_blocks, precision=highest_mode)
    orthonormal = jax.vmap(orthonormal_cols)(left_total)
    right_sum = jnp.einsum('adtk,tdr->tkr', merged, orthonormal, precision=highest_mode)
    right_new = right_sum / N_DP
    approx = jnp.einsum('tdr,tkr->dtk', orthonormal, right_new, precision=highest_mode)
    error_new = (merged - approx[None]).reshape(N_DP * D, KV).astype(jnp.bfloat16)
    grads_split = key_grad.reshape(TOKENS, N_TENSOR, head_block)
    weight_split = key_weight.reshape(D, N_TENSOR, head_block)
    input_grad = jnp.zeros((TOKENS, D), jnp.float32)
    for block_index in range(N_TENSOR):
        partial_value = jnp.dot(grads_split[:, block_index].astype(jnp.float32), weight_split[:, block_index].T.astype(jnp.float32), preferred_element_type=jnp.float32)
        rounded = lax.optimization_barrier(partial_value.astype(jnp.bfloat16))
        input_grad = input_grad + rounded.astype(jnp.float32)
    return (input_grad.astype(jnp.bfloat16), right_new.reshape(KV, RANK), error_new)
```

```python
import jax
import jax.numpy as jnp
from jax import lax
from jax.experimental import pallas as pl
from jax.experimental.pallas import tpu as pltpu
from jax.sharding import PartitionSpec as P

MESH = pl.DeviceIdType.MESH
HIGHEST = lax.Precision.HIGHEST
F32, BF16 = jnp.float32, jnp.bfloat16

TOK = 512
D = 4096
COLS = 512
RANK = 64
PIECES = 16
WIDE = D // PIECES
EARLY = 6

ACT = 0
YSEND = ACT + PIECES
KX, KI, KZ, KY, KS = YSEND + 1, YSEND + 2, YSEND + 3, YSEND + 6, YSEND + 9
LS, LY, LZ, LX = KS + 1, KS + 2, KS + 5, KS + 8
GZ, GY, GS = LX + 3, LX + 6, LX + 9
KG = GS + 1
RS, RY, RZ, RI = KG + 2, KG + 3, KG + 6, KG + 9
BZ, BY, BS = RI + 1, RI + 4, RI + 7
N_COPIES = BS + 1


def halves(value):
    high = value.astype(BF16)
    return high, (value - high.astype(F32)).astype(BF16)


def stacked(value):
    return jnp.concatenate(halves(value), axis=0)


def folded(value):
    half = value.shape[0] // 2
    return value[:half] + value[half:]


def dot(a, b, dims=((1,), (0,)), precision=None):
    return lax.dot_general(a, b, (dims, ((), ())), precision=precision, preferred_element_type=F32)


NT = ((1,), (1,))
TN = ((0,), (0,))


def kernel(
    act_in, grad_in, weight_in, error_in, right_in,
    input_grad, right_out, error_out,
    act, act_far, error, grad, grad_far, weight, weight_far, right,
    right_st, y_st, y_own, y_far, left_part, sib_in, left_half, y_in, left_y, z_in, left_z, x_in,
    left, aug, low_inv, ortho_st, ortho_nat, merged, err_stage, grad_stage, acc, acc_far,
    r0, r_sib, r1, r_y, r2, r_z, r3, r_i, right_full, right_fin,
    load_sem, store_sem, send_sem, recv_sem,
):
    dp, ten = lax.axis_index("dp"), lax.axis_index("tensor")
    z, y = lax.div(dp, 16), lax.rem(lax.div(dp, 4), 4)
    x_lo, core = lax.rem(lax.div(dp, 2), 2), lax.rem(dp, 2)
    other = 1 - ten

    def ring(pos, k):
        return lax.rem(pos + k + 4, 4)

    def peer(name, k=0):
        flipped = dp + 2 - 4 * x_lo
        if name == "S":
            return (dp + 1 - 2 * core, ten)
        if name == "I":
            return (flipped, ten)
        if name == "X":
            return (flipped, other)
        if name == "P":
            return (dp, other)
        if name == "Y":
            return (dp + 4 * (ring(y, k) - y), ten)
        return (dp + 16 * (ring(z, k) - z), ten)

    def remote(n, src, dst, to):
        return pltpu.make_async_remote_copy(
            src_ref=src, dst_ref=dst, send_sem=send_sem.at[n], recv_sem=recv_sem.at[n],
            device_id=to, device_id_type=MESH,
        )

    def send(n, src, dst, to):
        remote(n, src, dst, to).start()

    def arrived(n, dst):
        remote(n, dst, dst, peer("P")).wait_recv()

    def sent(n, src):
        remote(n, src, src, peer("P")).wait_send()

    def at(start, size):
        return pl.ds(pl.multiple_of(start, size), size)

    loads = [
        pltpu.make_async_copy(src, dst, load_sem.at[n])
        for n, (src, dst) in enumerate(
            ((right_in, right), (grad_in, grad), (act_in, act), (error_in, error), (weight_in, weight))
        )
    ]
    for load in loads:
        load.start()

    partners = [peer(name) for name in ("S", "I", "X", "P")]
    partners += [peer(name, k) for name in ("Y", "Z") for k in (1, 2, 3)]
    barrier = pltpu.get_barrier_semaphore()
    for to in partners:
        pl.semaphore_signal(barrier, inc=1, device_id=to, device_id_type=MESH)
    pl.semaphore_wait(barrier, len(partners))

    def act_chunk(n):
        return pl.ds(n * WIDE, WIDE)

    def send_act(n):
        send(ACT + n, act_in.at[:, act_chunk(n)], act_far.at[:, act_chunk(n)], peer("P"))

    k_base = core * 2048 + y * 512 + z * 128
    k_mine, k_next = at(k_base + x_lo * 64, 64), at(k_base + (1 - x_lo) * 64, 64)
    send(KX, weight_in.at[k_next, :], weight_far.at[k_next, :], peer("X"))
    send_act(0)

    own, far = at(ten * TOK, TOK), at(other * TOK, TOK)
    loads[0].wait()
    loads[1].wait()
    right_st[...] = stacked(right[...])
    y_own[...] = folded(dot(right_st[...], grad[far, :], NT))
    send(YSEND, y_own, y_far, peer("P"))
    for n in range(1, EARLY):
        send_act(n)
    y_st[...] = stacked(folded(dot(right_st[...], grad[own, :], NT)))

    loads[2].wait()
    loads[3].wait()

    def left_own(c, carry):
        cols = at(c * 512, 512)
        part = dot(y_st[...], act[:, cols]) + dot(right_st[...], error[cols, :], NT)
        left_part[:RANK, cols] = folded(part)
        return carry

    lax.fori_loop(0, 8, left_own, 0)
    arrived(YSEND, y_far)
    y_st[...] = stacked(y_far[...])

    def left_other(c, carry):
        cols = at(c * 512, 512)
        left_part[RANK:, cols] = folded(dot(y_st[...], act[:, cols]))
        return carry

    lax.fori_loop(0, 8, left_other, 0)

    my_half, sib_half = at(core * 2048, 2048), at((1 - core) * 2048, 2048)
    send(LS, left_part.at[:, sib_half], sib_in, peer("S"))
    arrived(KX, weight_far.at[k_mine, :])
    send(KI, weight_far.at[k_mine, :], weight_far.at[k_mine, :], peer("I"))
    arrived(LS, sib_in)

    def add_sibling(c, carry):
        cols = at(c * 512, 512)
        left_half[:, cols] = left_part[:, at(core * 2048 + c * 512, 512)] + sib_in[:, cols]
        return carry

    lax.fori_loop(0, 4, add_sibling, 0)
    for k in (1, 2, 3):
        send(LY + k - 1, left_half.at[:, at(ring(y, k) * 512, 512)], y_in.at[k - 1], peer("Y", k))

    def merge_own(n, carry):
        cols = at(n * WIDE, WIDE)
        merged[cols, :] = error[cols, :].astype(F32) + dot(act[:, cols], grad[own, :], TN)
        return carry

    lax.fori_loop(0, 8, merge_own, 0)

    for k in (1, 2, 3):
        arrived(LY + k - 1, y_in.at[k - 1])
    left_y[...] = left_half[:, at(y * 512, 512)] + y_in[0] + y_in[1] + y_in[2]
    for k in (1, 2, 3):
        send(LZ + k - 1, left_y.at[:, at(ring(z, k) * 128, 128)], z_in.at[k - 1], peer("Z", k))
    lax.fori_loop(8, 12, merge_own, 0)
    for k in (1, 2, 3):
        arrived(LZ + k - 1, z_in.at[k - 1])
    left_z[...] = left_y[:, at(z * 128, 128)] + z_in[0] + z_in[1] + z_in[2]
    send(LX, left_z.at[:RANK], x_in.at[0], peer("I"))
    send(LX + 1, left_z.at[RANK:], x_in.at[1], peer("X"))
    send(LX + 2, left_z.at[RANK:], x_in.at[2], peer("P"))
    for n in range(EARLY, PIECES):
        send_act(n)
    half_tok = TOK // 2

    def kg_rows(n):
        return pl.ds(n * half_tok, half_tok)

    def send_kg(n):
        rows = at(other * TOK + n * half_tok, half_tok)
        send(KG + n, grad_in.at[rows, :], grad_far.at[kg_rows(n), :], peer("P"))

    send_kg(0)

    lax.fori_loop(12, 16, merge_own, 0)
    loads[4].wait()

    def input_own(c, carry):
        cols = at(c * 512, 512)
        grad_stage[:, cols] = dot(grad[own, :], weight[cols, :], NT).astype(BF16)
        return carry

    lax.fori_loop(0, 8, input_own, 0)

    for k in range(3):
        arrived(LX + k, x_in.at[k])
    col_z = at(core * 2048 + y * 512 + z * 128, 128)
    left[:, col_z] = left_z[:RANK, :] + x_in[0] + x_in[1] + x_in[2]
    for k in (1, 2, 3):
        send(GZ + k - 1, left.at[:, col_z], left.at[:, col_z], peer("Z", k))
    for k in (1, 2, 3):
        arrived(GZ + k - 1, left.at[:, at(core * 2048 + y * 512 + ring(z, -k) * 128, 128)])
    col_y = at(core * 2048 + y * 512, 512)
    for k in (1, 2, 3):
        send(GY + k - 1, left.at[:, col_y], left.at[:, col_y], peer("Y", k))
    arrived(KI, weight_far.at[k_next, :])
    row_z = at(k_base, 128)
    for k in (1, 2, 3):
        send(KZ + k - 1, weight_far.at[row_z, :], weight_far.at[row_z, :], peer("Z", k))
    for k in (1, 2, 3):
        arrived(GY + k - 1, left.at[:, at(core * 2048 + ring(y, -k) * 512, 512)])
    send(GS, left.at[:, my_half], left.at[:, my_half], peer("S"))
    for k in (1, 2, 3):
        arrived(KZ + k - 1, weight_far.at[at(core * 2048 + y * 512 + ring(z, -k) * 128, 128), :])
    for k in (1, 2, 3):
        send(KY + k - 1, weight_far.at[col_y, :], weight_far.at[col_y, :], peer("Y", k))
    arrived(GS, left.at[:, sib_half])

    def gram_step(c, total):
        part = left[:, at(c * 512, 512)]
        return total + dot(part, part, NT, HIGHEST)

    aug[:, :RANK] = lax.fori_loop(0, 8, gram_step, jnp.zeros((RANK, RANK), F32))
    sub = lax.broadcasted_iota(jnp.int32, (RANK, 2 * RANK), 0)
    lane = lax.broadcasted_iota(jnp.int32, (RANK, 2 * RANK), 1)
    aug[:, RANK:] = (sub == lane).astype(F32)[:, :RANK]

    def eliminate(j, carry):
        mat, pivots = carry
        row = jnp.sum(jnp.where(sub == j, mat, 0.0), axis=0, keepdims=True)
        col = jnp.sum(jnp.where(lane == j, mat, 0.0), axis=1, keepdims=True)
        pivot = jnp.sum(jnp.where(lane[:1] == j, row, 0.0), axis=1, keepdims=True)
        pivots = jnp.where(sub == j, pivot, pivots)
        factor = jnp.where(sub > j, col / pivot, 0.0)
        return mat - factor * row, pivots

    mat, pivots = lax.fori_loop(0, RANK, eliminate, (aug[...], jnp.ones((RANK, 2 * RANK), F32)))
    aug[...] = mat / jnp.sqrt(pivots)
    low_inv[...] = aug[:, RANK:]

    def ortho_step(c, carry):
        cols = at(c * 512, 512)
        high, low = halves(dot(low_inv[...], left[:, cols], precision=HIGHEST))
        ortho_st[:RANK, cols] = high
        ortho_st[RANK:, cols] = low
        four = jnp.concatenate((high, low, high, jnp.zeros_like(high)), axis=0)
        ortho_nat[cols, :] = four.T
        return carry

    lax.fori_loop(0, 8, ortho_step, 0)

    acc[...] = jnp.zeros_like(acc)
    acc_far[...] = jnp.zeros_like(acc_far)

    def right_own(c, carry):
        cols = at(c * 512, 512)
        acc[...] += dot(ortho_st[:, cols], act[:, cols], NT)
        return carry

    lax.fori_loop(0, 8, right_own, 0)
    y_st[...] = stacked(folded(acc[...]))
    acc[...] = dot(y_st[...], grad[own, :])

    def right_error(c, carry):
        cols = at(c * 512, 512)
        acc[...] += dot(ortho_st[:, cols], error[cols, :])
        return carry

    lax.fori_loop(0, 8, right_error, 0)

    def merge_far(n, carry):
        cols = at(n * WIDE, WIDE)
        arrived(ACT + n, act_far.at[:, cols])
        piece = act_far[:, cols]
        merged[cols, :] += dot(piece, grad[far, :], TN)
        acc_far[...] += dot(ortho_st[:, cols], piece, NT)
        return carry

    lax.fori_loop(0, 12, merge_far, 0)
    for k in (1, 2, 3):
        arrived(KY + k - 1, weight_far.at[at(core * 2048 + ring(y, -k) * 512, 512), :])
    send(KS, weight_far.at[my_half, :], weight_far.at[my_half, :], peer("S"))
    lax.fori_loop(12, PIECES, merge_far, 0)
    y_st[...] = stacked(folded(acc_far[...]))
    r0[...] = folded(acc[...] + dot(y_st[...], grad[far, :]))

    r_mine, r_other = at(core * 256, 256), at((1 - core) * 256, 256)
    send(RS, r0.at[:, r_other], r_sib, peer("S"))
    arrived(KS, weight_far.at[sib_half, :])
    arrived(RS, r_sib)
    r1[...] = r0[:, r_mine] + r_sib[...]
    for k in (1, 2, 3):
        send(RY + k - 1, r1.at[at(ring(y, k) * 16, 16), :], r_y.at[k - 1], peer("Y", k))
    for k in (1, 2, 3):
        arrived(RY + k - 1, r_y.at[k - 1])
    r2[...] = r1[at(y * 16, 16), :] + r_y[0] + r_y[1] + r_y[2]

    def z_block(pos):
        return at(lax.div(pos, 2) * 8, 8), at(lax.rem(pos, 2) * 128, 128)

    for k in (1, 2, 3):
        rows, cols = z_block(ring(z, k))
        send(RZ + k - 1, r2.at[rows, cols], r_z.at[k - 1], peer("Z", k))
    for k in (1, 2, 3):
        arrived(RZ + k - 1, r_z.at[k - 1])
    rows, cols = z_block(z)
    r3[...] = r2[rows, cols] + r_z[0] + r_z[1] + r_z[2]
    send(RI, r3, r_i, peer("I"))
    send_kg(1)

    def store_grad(n, c):
        place = (kg_rows(n), at(c * 512, 512))
        return pltpu.make_async_copy(grad_stage.at[*place], input_grad.at[*place], store_sem.at[n])

    def input_far(n, c):
        rows, cols = kg_rows(n), at(c * 512, 512)
        term = dot(grad_far[rows, :], weight_far[cols, :], NT).astype(BF16)
        grad_stage[rows, cols] = (grad_stage[rows, cols].astype(F32) + term.astype(F32)).astype(BF16)
        store_grad(n, c).start()

    def input_first(c, carry):
        input_far(0, c)
        return carry

    def input_second(c, carry):
        input_far(1, c)
        return carry

    arrived(KG, grad_far.at[kg_rows(0), :])
    lax.fori_loop(0, 4, input_first, 0)
    arrived(RI, r_i)

    def full_block(py, pz):
        rows, cols = z_block(pz)
        return (
            at(py * 16 + lax.div(pz, 2) * 8, 8),
            at(core * 256 + lax.rem(pz, 2) * 128, 128),
        )

    rows, cols = full_block(y, z)
    right_full[rows, cols] = (r3[...] + r_i[...]) * (1.0 / 64.0)
    for k in (1, 2, 3):
        send(BZ + k - 1, right_full.at[rows, cols], right_full.at[rows, cols], peer("Z", k))
    lax.fori_loop(4, 6, input_first, 0)
    for k in (1, 2, 3):
        rows_in, cols_in = full_block(y, ring(z, -k))
        arrived(BZ + k - 1, right_full.at[rows_in, cols_in])
    rows = at(y * 16, 16)
    for k in (1, 2, 3):
        send(BY + k - 1, right_full.at[rows, r_mine], right_full.at[rows, r_mine], peer("Y", k))
    lax.fori_loop(6, 8, input_first, 0)
    for k in (1, 2, 3):
        arrived(BY + k - 1, right_full.at[at(ring(y, -k) * 16, 16), r_mine])
    send(BS, right_full.at[:, r_mine], right_full.at[:, r_mine], peer("S"))
    arrived(BS, right_full.at[:, r_other])
    right_out[...] = right_full[...]
    high, low = halves(right_full[...])
    right_fin[...] = jnp.concatenate((high, high, low, jnp.zeros_like(high)), axis=0)

    def store_error(n):
        rows = at(n * 256, 256)
        return pltpu.make_async_copy(err_stage.at[rows, :], error_out.at[rows, :], store_sem.at[2])

    def finish(n, carry):
        rows = at(n * 256, 256)
        err_stage[rows, :] = (merged[rows, :] - dot(ortho_nat[rows, :], right_fin[...])).astype(BF16)
        store_error(n).start()
        return carry

    lax.fori_loop(0, 16, finish, 0)
    arrived(KG + 1, grad_far.at[kg_rows(1), :])
    lax.fori_loop(0, 8, input_second, 0)

    for n in range(2):
        pltpu.make_async_copy(grad_stage.at[kg_rows(n), :], input_grad.at[kg_rows(n), :], store_sem.at[n]).wait()
    pltpu.make_async_copy(err_stage, error_out, store_sem.at[2]).wait()

    sources = {YSEND: y_own, KX: weight_far.at[k_next, :], KI: weight_far.at[k_mine, :], KS: weight_far.at[my_half, :],
               LS: left_part.at[:, sib_half], LX: left_z.at[:RANK], LX + 1: left_z.at[RANK:], LX + 2: left_z.at[RANK:],
               GS: left.at[:, my_half], RS: r0.at[:, r_other], RI: r3, BS: right_full.at[:, r_mine]}
    for n in range(PIECES):
        sources[ACT + n] = act_in.at[:, act_chunk(n)]
    for n in range(2):
        sources[KG + n] = grad_in.at[at(other * TOK + n * half_tok, half_tok), :]
    for k in (1, 2, 3):
        sources[KZ + k - 1] = weight_far.at[row_z, :]
        sources[KY + k - 1] = weight_far.at[col_y, :]
        sources[LY + k - 1] = left_half.at[:, at(ring(y, k) * 512, 512)]
        sources[LZ + k - 1] = left_y.at[:, at(ring(z, k) * 128, 128)]
        sources[GZ + k - 1] = left.at[:, col_z]
        sources[GY + k - 1] = left.at[:, col_y]
        sources[RY + k - 1] = r1.at[at(ring(y, k) * 16, 16), :]
        sources[RZ + k - 1] = r2.at[z_block(ring(z, k))]
        sources[BZ + k - 1] = right_full.at[full_block(y, z)]
        sources[BY + k - 1] = right_full.at[rows, r_mine]
    for n in range(N_COPIES):
        sent(n, sources[n])


def shards(activations, key_grad, key_weight, error_prev, right_prev):
    def vmem(*shape, kind=F32):
        return pltpu.VMEM(shape, kind)

    input_grad, right_new, error_new = pl.pallas_call(
        kernel,
        out_shape=(
            jax.ShapeDtypeStruct((TOK, D), BF16),
            jax.ShapeDtypeStruct((RANK, COLS), F32),
            jax.ShapeDtypeStruct((D, COLS), BF16),
        ),
        in_specs=[pl.BlockSpec(memory_space=pl.ANY)] * 5,
        out_specs=(
            pl.BlockSpec(memory_space=pl.ANY),
            pl.BlockSpec(memory_space=pltpu.VMEM),
            pl.BlockSpec(memory_space=pl.ANY),
        ),
        scratch_shapes=[
            vmem(TOK, D, kind=BF16),
            vmem(TOK, D, kind=BF16),
            vmem(D, COLS, kind=BF16),
            vmem(2 * TOK, COLS, kind=BF16),
            vmem(TOK, COLS, kind=BF16),
            vmem(D, COLS, kind=BF16),
            vmem(D, COLS, kind=BF16),
            vmem(RANK, COLS),
            vmem(2 * RANK, COLS, kind=BF16),
            vmem(2 * RANK, TOK, kind=BF16),
            vmem(RANK, TOK),
            vmem(RANK, TOK),
            vmem(2 * RANK, D),
            vmem(2 * RANK, D // 2),
            vmem(2 * RANK, D // 2),
            vmem(3, 2 * RANK, 512),
            vmem(2 * RANK, 512),
            vmem(3, 2 * RANK, 128),
            vmem(2 * RANK, 128),
            vmem(3, RANK, 128),
            vmem(RANK, D),
            vmem(RANK, 2 * RANK),
            vmem(RANK, RANK),
            vmem(2 * RANK, D, kind=BF16),
            vmem(D, 4 * RANK, kind=BF16),
            vmem(D, COLS),
            vmem(D, COLS, kind=BF16),
            vmem(TOK, D, kind=BF16),
            vmem(2 * RANK, COLS),
            vmem(2 * RANK, TOK),
            vmem(RANK, COLS),
            vmem(RANK, 256),
            vmem(RANK, 256),
            vmem(3, 16, 256),
            vmem(16, 256),
            vmem(3, 8, 128),
            vmem(8, 128),
            vmem(8, 128),
            vmem(RANK, COLS),
            vmem(4 * RANK, COLS, kind=BF16),
            pltpu.SemaphoreType.DMA((5,)),
            pltpu.SemaphoreType.DMA((3,)),
            pltpu.SemaphoreType.DMA((N_COPIES,)),
            pltpu.SemaphoreType.DMA((N_COPIES,)),
        ],
        compiler_params=pltpu.CompilerParams(
            collective_id=0, has_side_effects=True, vmem_limit_bytes=60 * 2**20
        ),
    )(activations, key_grad, key_weight, error_prev, right_prev.T)
    return input_grad, right_new.T, error_new


def solution(mesh):
    placed = (
        P(("dp", "tensor"), None),
        P("dp", "tensor"),
        P(None, "tensor"),
        P("dp", "tensor"),
        P("tensor", None),
    )
    return jax.shard_map(
        shards,
        mesh=mesh,
        in_specs=placed,
        out_specs=(P(("dp", "tensor"), None), P("tensor", None), P("dp", "tensor")),
        check_vma=False,
    )
```

```python
import jax
import jax.numpy as jnp
from jax import lax
from jax.experimental import pallas as pl
from jax.experimental.pallas import tpu as pltpu
from jax.sharding import PartitionSpec as P

MESH = pl.DeviceIdType.MESH
HIGHEST = lax.Precision.HIGHEST
F32, BF16 = jnp.float32, jnp.bfloat16

TOK = 512
D = 4096
COLS = 512
RANK = 64
PIECES = 16
WIDE = D // PIECES
EARLY = 6

PEERS = 15
ACT = 0
YSEND = ACT + PIECES
KX, KZ, KS = YSEND + 1, YSEND + 2, YSEND + 2 + PEERS
LS, LZ, LX = KS + 1, KS + 2, KS + 2 + PEERS
GZ, GS = LX + 3, LX + 3 + PEERS
KG = GS + 1
RS, RZ, RI = KG + 2, KG + 3, KG + 3 + PEERS
BZ, BS = RI + 1, RI + 1 + PEERS
N_COPIES = BS + 1


def halves(value):
    high = value.astype(BF16)
    return high, (value - high.astype(F32)).astype(BF16)


def stacked(value):
    return jnp.concatenate(halves(value), axis=0)


def folded(value):
    half = value.shape[0] // 2
    return value[:half] + value[half:]


def dot(a, b, dims=((1,), (0,)), precision=None):
    return lax.dot_general(a, b, (dims, ((), ())), precision=precision, preferred_element_type=F32)


NT = ((1,), (1,))
TN = ((0,), (0,))


def kernel(
    act_in, grad_in, weight_in, error_in, right_in,
    input_grad, right_out, error_out,
    act, act_far, error, grad, grad_far, weight, weight_far, right,
    right_st, y_st, y_own, y_far, left_part, sib_in, left_half, plane_in, left_z, x_in,
    left, aug, low_inv, ortho_st, ortho_nat, merged, err_stage, grad_stage, acc, acc_far,
    r0, r_sib, r1, r_in, r3, r_i, right_full, right_fin,
    load_sem, store_sem, send_sem, recv_sem,
):
    dp, ten = lax.axis_index("dp"), lax.axis_index("tensor")
    z, y = lax.div(dp, 16), lax.rem(lax.div(dp, 4), 4)
    x_lo, core = lax.rem(lax.div(dp, 2), 2), lax.rem(dp, 2)
    other = 1 - ten

    def plane(k, sign=1):
        return lax.rem(y + sign * lax.div(k, 4) + 4, 4), lax.rem(z + sign * lax.rem(k, 4) + 4, 4)

    def peer(name, k=0):
        flipped = dp + 2 - 4 * x_lo
        if name == "S":
            return (dp + 1 - 2 * core, ten)
        if name == "I":
            return (flipped, ten)
        if name == "X":
            return (flipped, other)
        if name == "P":
            return (dp, other)
        py, pz = plane(k)
        return (dp + 4 * (py - y) + 16 * (pz - z), ten)

    def remote(n, src, dst, to):
        return pltpu.make_async_remote_copy(
            src_ref=src, dst_ref=dst, send_sem=send_sem.at[n], recv_sem=recv_sem.at[n],
            device_id=to, device_id_type=MESH,
        )

    def send(n, src, dst, to):
        remote(n, src, dst, to).start()

    def arrived(n, dst):
        remote(n, dst, dst, peer("P")).wait_recv()

    def sent(n, src):
        remote(n, src, src, peer("P")).wait_send()

    def plane_send(base, src, dst):
        def one(k, carry):
            send(base + k - 1, src(*plane(k)), dst(k - 1), peer("plane", k))
            return carry

        lax.fori_loop(1, PEERS + 1, one, 0)

    def plane_arrived(base, dst):
        def one(k, carry):
            arrived(base + k - 1, dst(k - 1, *plane(k, -1)))
            return carry

        lax.fori_loop(1, PEERS + 1, one, 0)

    def plane_sent(base, src):
        def one(k, carry):
            sent(base + k - 1, src(*plane(k)))
            return carry

        lax.fori_loop(1, PEERS + 1, one, 0)

    def at(start, size):
        return pl.ds(pl.multiple_of(start, size), size)

    loads = [
        pltpu.make_async_copy(src, dst, load_sem.at[n])
        for n, (src, dst) in enumerate(
            ((right_in, right), (grad_in, grad), (act_in, act), (error_in, error), (weight_in, weight))
        )
    ]
    for load in loads:
        load.start()

    partners = [peer(name) for name in ("S", "I", "X", "P")]
    partners += [peer("plane", k) for k in range(1, PEERS + 1)]
    barrier = pltpu.get_barrier_semaphore()
    for to in partners:
        pl.semaphore_signal(barrier, inc=1, device_id=to, device_id_type=MESH)
    pl.semaphore_wait(barrier, len(partners))

    def act_chunk(n):
        return pl.ds(n * WIDE, WIDE)

    def send_act(n):
        send(ACT + n, act_in.at[:, act_chunk(n)], act_far.at[:, act_chunk(n)], peer("P"))

    k_rows = at(core * 2048 + y * 512 + z * 128, 128)
    send(KX, weight_in.at[k_rows, :], weight_far.at[k_rows, :], peer("X"))
    send_act(0)

    own, far = at(ten * TOK, TOK), at(other * TOK, TOK)
    loads[0].wait()
    loads[1].wait()
    right_st[...] = stacked(right[...])
    y_own[...] = folded(dot(right_st[...], grad[far, :], NT))
    send(YSEND, y_own, y_far, peer("P"))
    for n in range(1, EARLY):
        send_act(n)
    y_st[...] = stacked(folded(dot(right_st[...], grad[own, :], NT)))

    loads[2].wait()
    loads[3].wait()

    def left_own(c, carry):
        cols = at(c * 512, 512)
        part = dot(y_st[...], act[:, cols]) + dot(right_st[...], error[cols, :], NT)
        left_part[:RANK, cols] = folded(part)
        return carry

    lax.fori_loop(0, 8, left_own, 0)
    arrived(YSEND, y_far)
    y_st[...] = stacked(y_far[...])

    def left_other(c, carry):
        cols = at(c * 512, 512)
        left_part[RANK:, cols] = folded(dot(y_st[...], act[:, cols]))
        return carry

    lax.fori_loop(0, 8, left_other, 0)

    my_half, sib_half = at(core * 2048, 2048), at((1 - core) * 2048, 2048)
    send(LS, left_part.at[:, sib_half], sib_in, peer("S"))
    arrived(LS, sib_in)

    def add_sibling(c, carry):
        cols = at(c * 512, 512)
        left_half[:, cols] = left_part[:, at(core * 2048 + c * 512, 512)] + sib_in[:, cols]
        return carry

    lax.fori_loop(0, 4, add_sibling, 0)
    def plane_cols(py, pz):
        return at(py * 512 + pz * 128, 128)

    plane_send(LZ, lambda py, pz: left_half.at[:, plane_cols(py, pz)], lambda n: plane_in.at[n])

    def merge_own(n, carry):
        cols = at(n * WIDE, WIDE)
        merged[cols, :] = error[cols, :].astype(F32) + dot(act[:, cols], grad[own, :], TN)
        return carry

    lax.fori_loop(0, 12, merge_own, 0)
    plane_arrived(LZ, lambda n, py, pz: plane_in.at[n])

    def add_plane(n, total):
        return total + plane_in[n]

    left_z[...] = lax.fori_loop(0, PEERS, add_plane, left_half[:, plane_cols(y, z)])
    send(LX, left_z.at[:RANK], x_in.at[0], peer("I"))
    send(LX + 1, left_z.at[RANK:], x_in.at[1], peer("X"))
    send(LX + 2, left_z.at[RANK:], x_in.at[2], peer("P"))
    for n in range(EARLY, PIECES):
        send_act(n)
    half_tok = TOK // 2

    def kg_rows(n):
        return pl.ds(n * half_tok, half_tok)

    def send_kg(n):
        rows = at(other * TOK + n * half_tok, half_tok)
        send(KG + n, grad_in.at[rows, :], grad_far.at[kg_rows(n), :], peer("P"))

    send_kg(0)

    lax.fori_loop(12, 16, merge_own, 0)
    loads[4].wait()

    def input_own(c, carry):
        cols = at(c * 512, 512)
        grad_stage[:, cols] = dot(grad[own, :], weight[cols, :], NT).astype(BF16)
        return carry

    lax.fori_loop(0, 8, input_own, 0)

    for k in range(3):
        arrived(LX + k, x_in.at[k])
    def left_cols(py, pz):
        return at(core * 2048 + py * 512 + pz * 128, 128)

    col_z = left_cols(y, z)
    left[:, col_z] = left_z[:RANK, :] + x_in[0] + x_in[1] + x_in[2]
    plane_send(GZ, lambda py, pz: left.at[:, col_z], lambda n: left.at[:, col_z])
    plane_arrived(GZ, lambda n, py, pz: left.at[:, left_cols(py, pz)])
    send(GS, left.at[:, my_half], left.at[:, my_half], peer("S"))
    arrived(KX, weight_far.at[k_rows, :])
    plane_send(KZ, lambda py, pz: weight_far.at[k_rows, :], lambda n: weight_far.at[k_rows, :])
    arrived(GS, left.at[:, sib_half])

    def gram_step(c, total):
        part = left[:, at(c * 512, 512)]
        return total + dot(part, part, NT, HIGHEST)

    aug[:, :RANK] = lax.fori_loop(0, 8, gram_step, jnp.zeros((RANK, RANK), F32))
    sub = lax.broadcasted_iota(jnp.int32, (RANK, 2 * RANK), 0)
    lane = lax.broadcasted_iota(jnp.int32, (RANK, 2 * RANK), 1)
    aug[:, RANK:] = (sub == lane).astype(F32)[:, :RANK]

    def eliminate(j, carry):
        mat, pivots = carry
        row = jnp.sum(jnp.where(sub == j, mat, 0.0), axis=0, keepdims=True)
        col = jnp.sum(jnp.where(lane == j, mat, 0.0), axis=1, keepdims=True)
        pivot = jnp.sum(jnp.where(lane[:1] == j, row, 0.0), axis=1, keepdims=True)
        pivots = jnp.where(sub == j, pivot, pivots)
        factor = jnp.where(sub > j, col / pivot, 0.0)
        return mat - factor * row, pivots

    mat, pivots = lax.fori_loop(0, RANK, eliminate, (aug[...], jnp.ones((RANK, 2 * RANK), F32)))
    aug[...] = mat / jnp.sqrt(pivots)
    low_inv[...] = aug[:, RANK:]

    def ortho_step(c, carry):
        cols = at(c * 512, 512)
        high, low = halves(dot(low_inv[...], left[:, cols], precision=HIGHEST))
        ortho_st[:RANK, cols] = high
        ortho_st[RANK:, cols] = low
        four = jnp.concatenate((high, low, high, jnp.zeros_like(high)), axis=0)
        ortho_nat[cols, :] = four.T
        return carry

    lax.fori_loop(0, 8, ortho_step, 0)

    acc[...] = jnp.zeros_like(acc)
    acc_far[...] = jnp.zeros_like(acc_far)

    def right_own(c, carry):
        cols = at(c * 512, 512)
        acc[...] += dot(ortho_st[:, cols], act[:, cols], NT)
        return carry

    lax.fori_loop(0, 8, right_own, 0)
    y_st[...] = stacked(folded(acc[...]))
    acc[...] = dot(y_st[...], grad[own, :])

    def right_error(c, carry):
        cols = at(c * 512, 512)
        acc[...] += dot(ortho_st[:, cols], error[cols, :])
        return carry

    lax.fori_loop(0, 8, right_error, 0)

    def merge_far(n, carry):
        cols = at(n * WIDE, WIDE)
        arrived(ACT + n, act_far.at[:, cols])
        piece = act_far[:, cols]
        merged[cols, :] += dot(piece, grad[far, :], TN)
        acc_far[...] += dot(ortho_st[:, cols], piece, NT)
        return carry

    lax.fori_loop(0, 12, merge_far, 0)
    plane_arrived(KZ, lambda n, py, pz: weight_far.at[left_cols(py, pz), :])
    send(KS, weight_far.at[my_half, :], weight_far.at[my_half, :], peer("S"))
    lax.fori_loop(12, PIECES, merge_far, 0)
    y_st[...] = stacked(folded(acc_far[...]))
    r0[...] = folded(acc[...] + dot(y_st[...], grad[far, :]))

    r_mine, r_other = at(core * 256, 256), at((1 - core) * 256, 256)
    send(RS, r0.at[:, r_other], r_sib, peer("S"))
    arrived(KS, weight_far.at[sib_half, :])
    arrived(RS, r_sib)
    r1[...] = r0[:, r_mine] + r_sib[...]

    def right_block(py, pz):
        return at(py * 16 + lax.div(pz, 2) * 8, 8), at(lax.rem(pz, 2) * 128, 128)

    plane_send(RZ, lambda py, pz: r1.at[right_block(py, pz)], lambda n: r_in.at[n])
    plane_arrived(RZ, lambda n, py, pz: r_in.at[n])

    def add_right(n, total):
        return total + r_in[n]

    r3[...] = lax.fori_loop(0, PEERS, add_right, r1[right_block(y, z)])
    send(RI, r3, r_i, peer("I"))
    send_kg(1)

    def store_grad(n, c):
        place = (kg_rows(n), at(c * 512, 512))
        return pltpu.make_async_copy(grad_stage.at[*place], input_grad.at[*place], store_sem.at[n])

    def input_far(n, c):
        rows, cols = kg_rows(n), at(c * 512, 512)
        term = dot(grad_far[rows, :], weight_far[cols, :], NT).astype(BF16)
        grad_stage[rows, cols] = (grad_stage[rows, cols].astype(F32) + term.astype(F32)).astype(BF16)
        store_grad(n, c).start()

    def input_first(c, carry):
        input_far(0, c)
        return carry

    def input_second(c, carry):
        input_far(1, c)
        return carry

    arrived(KG, grad_far.at[kg_rows(0), :])
    lax.fori_loop(0, 4, input_first, 0)
    arrived(RI, r_i)

    def full_block(py, pz):
        return (
            at(py * 16 + lax.div(pz, 2) * 8, 8),
            at(core * 256 + lax.rem(pz, 2) * 128, 128),
        )

    mine = full_block(y, z)
    right_full[mine] = (r3[...] + r_i[...]) * (1.0 / 64.0)
    plane_send(BZ, lambda py, pz: right_full.at[mine], lambda n: right_full.at[mine])
    lax.fori_loop(4, 8, input_first, 0)
    plane_arrived(BZ, lambda n, py, pz: right_full.at[full_block(py, pz)])
    send(BS, right_full.at[:, r_mine], right_full.at[:, r_mine], peer("S"))
    arrived(BS, right_full.at[:, r_other])
    right_out[...] = right_full[...]
    high, low = halves(right_full[...])
    right_fin[...] = jnp.concatenate((high, high, low, jnp.zeros_like(high)), axis=0)

    def store_error(n):
        rows = at(n * 256, 256)
        return pltpu.make_async_copy(err_stage.at[rows, :], error_out.at[rows, :], store_sem.at[2])

    def finish(n, carry):
        rows = at(n * 256, 256)
        err_stage[rows, :] = (merged[rows, :] - dot(ortho_nat[rows, :], right_fin[...])).astype(BF16)
        store_error(n).start()
        return carry

    lax.fori_loop(0, 16, finish, 0)
    arrived(KG + 1, grad_far.at[kg_rows(1), :])
    lax.fori_loop(0, 8, input_second, 0)

    for n in range(2):
        pltpu.make_async_copy(grad_stage.at[kg_rows(n), :], input_grad.at[kg_rows(n), :], store_sem.at[n]).wait()
    pltpu.make_async_copy(err_stage, error_out, store_sem.at[2]).wait()

    sources = {
        YSEND: y_own, KX: weight_in.at[k_rows, :], KS: weight_far.at[my_half, :],
        LS: left_part.at[:, sib_half], LX: left_z.at[:RANK], LX + 1: left_z.at[RANK:], LX + 2: left_z.at[RANK:],
        GS: left.at[:, my_half], RS: r0.at[:, r_other], RI: r3, BS: right_full.at[:, r_mine],
    }
    for n in range(PIECES):
        sources[ACT + n] = act_in.at[:, act_chunk(n)]
    for n in range(2):
        sources[KG + n] = grad_in.at[at(other * TOK + n * half_tok, half_tok), :]
    for n, src in sources.items():
        sent(n, src)
    plane_sent(KZ, lambda py, pz: weight_far.at[k_rows, :])
    plane_sent(LZ, lambda py, pz: left_half.at[:, plane_cols(py, pz)])
    plane_sent(GZ, lambda py, pz: left.at[:, col_z])
    plane_sent(RZ, lambda py, pz: r1.at[right_block(py, pz)])
    plane_sent(BZ, lambda py, pz: right_full.at[mine])


def shards(activations, key_grad, key_weight, error_prev, right_prev):
    def vmem(*shape, kind=F32):
        return pltpu.VMEM(shape, kind)

    input_grad, right_new, error_new = pl.pallas_call(
        kernel,
        out_shape=(
            jax.ShapeDtypeStruct((TOK, D), BF16),
            jax.ShapeDtypeStruct((RANK, COLS), F32),
            jax.ShapeDtypeStruct((D, COLS), BF16),
        ),
        in_specs=[pl.BlockSpec(memory_space=pl.ANY)] * 5,
        out_specs=(
            pl.BlockSpec(memory_space=pl.ANY),
            pl.BlockSpec(memory_space=pltpu.VMEM),
            pl.BlockSpec(memory_space=pl.ANY),
        ),
        scratch_shapes=[
            vmem(TOK, D, kind=BF16),
            vmem(TOK, D, kind=BF16),
            vmem(D, COLS, kind=BF16),
            vmem(2 * TOK, COLS, kind=BF16),
            vmem(TOK, COLS, kind=BF16),
            vmem(D, COLS, kind=BF16),
            vmem(D, COLS, kind=BF16),
            vmem(RANK, COLS),
            vmem(2 * RANK, COLS, kind=BF16),
            vmem(2 * RANK, TOK, kind=BF16),
            vmem(RANK, TOK),
            vmem(RANK, TOK),
            vmem(2 * RANK, D),
            vmem(2 * RANK, D // 2),
            vmem(2 * RANK, D // 2),
            vmem(PEERS, 2 * RANK, 128),
            vmem(2 * RANK, 128),
            vmem(3, RANK, 128),
            vmem(RANK, D),
            vmem(RANK, 2 * RANK),
            vmem(RANK, RANK),
            vmem(2 * RANK, D, kind=BF16),
            vmem(D, 4 * RANK, kind=BF16),
            vmem(D, COLS),
            vmem(D, COLS, kind=BF16),
            vmem(TOK, D, kind=BF16),
            vmem(2 * RANK, COLS),
            vmem(2 * RANK, TOK),
            vmem(RANK, COLS),
            vmem(RANK, 256),
            vmem(RANK, 256),
            vmem(PEERS, 8, 128),
            vmem(8, 128),
            vmem(8, 128),
            vmem(RANK, COLS),
            vmem(4 * RANK, COLS, kind=BF16),
            pltpu.SemaphoreType.DMA((5,)),
            pltpu.SemaphoreType.DMA((3,)),
            pltpu.SemaphoreType.DMA((N_COPIES,)),
            pltpu.SemaphoreType.DMA((N_COPIES,)),
        ],
        compiler_params=pltpu.CompilerParams(
            collective_id=0, has_side_effects=True, vmem_limit_bytes=60 * 2**20
        ),
    )(activations, key_grad, key_weight, error_prev, right_prev.T)
    return input_grad, right_new.T, error_new


def solution(mesh):
    placed = (
        P(("dp", "tensor"), None),
        P("dp", "tensor"),
        P(None, "tensor"),
        P("dp", "tensor"),
        P("tensor", None),
    )
    return jax.shard_map(
        shards,
        mesh=mesh,
        in_specs=placed,
        out_specs=(P(("dp", "tensor"), None), P("tensor", None), P("dp", "tensor")),
        check_vma=False,
    )
```

```python
import jax
import jax.numpy as jnp
from jax import lax
from jax.experimental import pallas as pl
from jax.experimental.pallas import tpu as pltpu
from jax.sharding import PartitionSpec as P

MESH = pl.DeviceIdType.MESH
HIGHEST = lax.Precision.HIGHEST
F32, BF16 = jnp.float32, jnp.bfloat16

TOK = 512
D = 4096
COLS = 512
RANK = 64
PIECES = 16
WIDE = D // PIECES
EARLY = 6

PEERS = 15
ACT = 0
YSEND = ACT + PIECES
KX, KZ, KS = YSEND + 1, YSEND + 2, YSEND + 2 + PEERS
LS, LZ, LX = KS + 1, KS + 2, KS + 2 + PEERS
GZ, GS = LX + 3, LX + 3 + PEERS
KG = GS + 1
RS, RZ, RI = KG + 2, KG + 3, KG + 3 + PEERS
BZ, BS = RI + 1, RI + 1 + PEERS
N_COPIES = BS + 1


def halves(value):
    high = value.astype(BF16)
    return high, (value - high.astype(F32)).astype(BF16)


def stacked(value):
    return jnp.concatenate(halves(value), axis=0)


def folded(value):
    half = value.shape[0] // 2
    return value[:half] + value[half:]


def dot(a, b, dims=((1,), (0,)), precision=None):
    return lax.dot_general(a, b, (dims, ((), ())), precision=precision, preferred_element_type=F32)


NT = ((1,), (1,))
TN = ((0,), (0,))


def kernel(
    act_in, grad_in, weight_in, error_in, right_in,
    input_grad, right_out, error_out,
    act, act_far, error, grad, grad_far, weight, weight_far, right,
    right_st, y_st, y_own, y_far, left_part, sib_in, left_half, plane_in, left_z, x_in,
    left, aug, low_inv, ortho_st, ortho_nat, merged, err_stage, grad_stage, acc, acc_far,
    r0, r_sib, r1, r_in, r3, r_i, right_full, right_fin,
    load_sem, store_sem, send_sem, recv_sem,
):
    dp, ten = lax.axis_index("dp"), lax.axis_index("tensor")
    z, y = lax.div(dp, 16), lax.rem(lax.div(dp, 4), 4)
    x_lo, core = lax.rem(lax.div(dp, 2), 2), lax.rem(dp, 2)
    other = 1 - ten

    def plane(k, sign=1):
        return lax.rem(y + sign * lax.div(k, 4) + 4, 4), lax.rem(z + sign * lax.rem(k, 4) + 4, 4)

    def peer(name, k=0):
        flipped = dp + 2 - 4 * x_lo
        if name == "S":
            return (dp + 1 - 2 * core, ten)
        if name == "I":
            return (flipped, ten)
        if name == "X":
            return (flipped, other)
        if name == "P":
            return (dp, other)
        py, pz = plane(k)
        return (dp + 4 * (py - y) + 16 * (pz - z), ten)

    def remote(n, src, dst, to):
        return pltpu.make_async_remote_copy(
            src_ref=src, dst_ref=dst, send_sem=send_sem.at[n], recv_sem=recv_sem.at[n],
            device_id=to, device_id_type=MESH,
        )

    def send(n, src, dst, to):
        remote(n, src, dst, to).start()

    def arrived(n, dst):
        remote(n, dst, dst, peer("P")).wait_recv()

    def sent(n, src):
        remote(n, src, src, peer("P")).wait_send()

    def plane_send(base, src, dst):
        def one(k, carry):
            send(base + k - 1, src(*plane(k)), dst(k - 1), peer("plane", k))
            return carry

        lax.fori_loop(1, PEERS + 1, one, 0)

    def plane_arrived(base, dst):
        def one(k, carry):
            arrived(base + k - 1, dst(k - 1, *plane(k, -1)))
            return carry

        lax.fori_loop(1, PEERS + 1, one, 0)

    def plane_sent(base, src):
        def one(k, carry):
            sent(base + k - 1, src(*plane(k)))
            return carry

        lax.fori_loop(1, PEERS + 1, one, 0)

    def at(start, size):
        return pl.ds(pl.multiple_of(start, size), size)

    loads = [
        pltpu.make_async_copy(src, dst, load_sem.at[n])
        for n, (src, dst) in enumerate(
            ((right_in, right), (grad_in, grad), (act_in, act), (error_in, error), (weight_in, weight))
        )
    ]
    for load in loads:
        load.start()

    partners = [peer(name) for name in ("S", "I", "X", "P")]
    partners += [peer("plane", k) for k in range(1, PEERS + 1)]
    barrier = pltpu.get_barrier_semaphore()
    for to in partners:
        pl.semaphore_signal(barrier, inc=1, device_id=to, device_id_type=MESH)
    pl.semaphore_wait(barrier, len(partners))

    def act_chunk(n):
        return pl.ds(n * WIDE, WIDE)

    def send_act(n):
        send(ACT + n, act_in.at[:, act_chunk(n)], act_far.at[:, act_chunk(n)], peer("P"))

    k_rows = at(core * 2048 + y * 512 + z * 128, 128)
    send(KX, weight_in.at[k_rows, :], weight_far.at[k_rows, :], peer("P"))
    send_act(0)

    own, far = at(ten * TOK, TOK), at(other * TOK, TOK)
    loads[0].wait()
    loads[1].wait()
    right_st[...] = stacked(right[...])
    y_own[...] = folded(dot(right_st[...], grad[far, :], NT))
    send(YSEND, y_own, y_far, peer("P"))
    for n in range(1, EARLY):
        send_act(n)
    y_st[...] = stacked(folded(dot(right_st[...], grad[own, :], NT)))

    loads[2].wait()
    loads[3].wait()

    def left_own(c, carry):
        cols = at(c * 512, 512)
        part = dot(y_st[...], act[:, cols]) + dot(right_st[...], error[cols, :], NT)
        left_part[:RANK, cols] = folded(part)
        return carry

    lax.fori_loop(0, 8, left_own, 0)
    arrived(YSEND, y_far)
    y_st[...] = stacked(y_far[...])

    def left_other(c, carry):
        cols = at(c * 512, 512)
        left_part[RANK:, cols] = folded(dot(y_st[...], act[:, cols]))
        return carry

    lax.fori_loop(0, 8, left_other, 0)

    my_half, sib_half = at(core * 2048, 2048), at((1 - core) * 2048, 2048)
    send(LS, left_part.at[:, sib_half], sib_in, peer("S"))
    arrived(LS, sib_in)

    def add_sibling(c, carry):
        cols = at(c * 512, 512)
        left_half[:, cols] = left_part[:, at(core * 2048 + c * 512, 512)] + sib_in[:, cols]
        return carry

    lax.fori_loop(0, 4, add_sibling, 0)
    def plane_cols(py, pz):
        return at(py * 512 + pz * 128, 128)

    plane_send(LZ, lambda py, pz: left_half.at[:, plane_cols(py, pz)], lambda n: plane_in.at[n])

    def merge_own(n, carry):
        cols = at(n * WIDE, WIDE)
        merged[cols, :] = error[cols, :].astype(F32) + dot(act[:, cols], grad[own, :], TN)
        return carry

    lax.fori_loop(0, 12, merge_own, 0)
    plane_arrived(LZ, lambda n, py, pz: plane_in.at[n])

    def add_plane(n, total):
        return total + plane_in[n]

    left_z[...] = lax.fori_loop(0, PEERS, add_plane, left_half[:, plane_cols(y, z)])
    send(LX, left_z.at[:RANK], x_in.at[0], peer("I"))
    send(LX + 1, left_z.at[RANK:], x_in.at[1], peer("X"))
    send(LX + 2, left_z.at[RANK:], x_in.at[2], peer("P"))
    for n in range(EARLY, PIECES):
        send_act(n)
    half_tok = TOK // 2

    def kg_rows(n):
        return pl.ds(n * half_tok, half_tok)

    def send_kg(n):
        rows = at(other * TOK + n * half_tok, half_tok)
        send(KG + n, grad_in.at[rows, :], grad_far.at[kg_rows(n), :], peer("P"))

    send_kg(0)

    lax.fori_loop(12, 16, merge_own, 0)
    loads[4].wait()

    def input_own(c, carry):
        cols = at(c * 512, 512)
        grad_stage[:, cols] = dot(grad[own, :], weight[cols, :], NT).astype(BF16)
        return carry

    lax.fori_loop(0, 8, input_own, 0)

    for k in range(3):
        arrived(LX + k, x_in.at[k])
    def left_cols(py, pz):
        return at(core * 2048 + py * 512 + pz * 128, 128)

    col_z = left_cols(y, z)
    left[:, col_z] = left_z[:RANK, :] + x_in[0] + x_in[1] + x_in[2]
    plane_send(GZ, lambda py, pz: left.at[:, col_z], lambda n: left.at[:, col_z])
    plane_arrived(GZ, lambda n, py, pz: left.at[:, left_cols(py, pz)])
    send(GS, left.at[:, my_half], left.at[:, my_half], peer("S"))
    arrived(KX, weight_far.at[k_rows, :])
    plane_send(KZ, lambda py, pz: weight_far.at[k_rows, :], lambda n: weight_far.at[k_rows, :])
    arrived(GS, left.at[:, sib_half])

    def gram_step(c, total):
        part = left[:, at(c * 512, 512)]
        return total + dot(part, part, NT, HIGHEST)

    aug[:, :RANK] = lax.fori_loop(0, 8, gram_step, jnp.zeros((RANK, RANK), F32))
    sub = lax.broadcasted_iota(jnp.int32, (RANK, 2 * RANK), 0)
    lane = lax.broadcasted_iota(jnp.int32, (RANK, 2 * RANK), 1)
    aug[:, RANK:] = (sub == lane).astype(F32)[:, :RANK]

    def eliminate(j, carry):
        mat, pivots = carry
        row = jnp.sum(jnp.where(sub == j, mat, 0.0), axis=0, keepdims=True)
        col = jnp.sum(jnp.where(lane == j, mat, 0.0), axis=1, keepdims=True)
        pivot = jnp.sum(jnp.where(lane[:1] == j, row, 0.0), axis=1, keepdims=True)
        pivots = jnp.where(sub == j, pivot, pivots)
        factor = jnp.where(sub > j, col / pivot, 0.0)
        return mat - factor * row, pivots

    mat, pivots = lax.fori_loop(0, RANK, eliminate, (aug[...], jnp.ones((RANK, 2 * RANK), F32)))
    aug[...] = mat / jnp.sqrt(pivots)
    low_inv[...] = aug[:, RANK:]

    def ortho_step(c, carry):
        cols = at(c * 512, 512)
        high, low = halves(dot(low_inv[...], left[:, cols], precision=HIGHEST))
        ortho_st[:RANK, cols] = high
        ortho_st[RANK:, cols] = low
        four = jnp.concatenate((high, low, high, jnp.zeros_like(high)), axis=0)
        ortho_nat[cols, :] = four.T
        return carry

    lax.fori_loop(0, 8, ortho_step, 0)

    acc[...] = jnp.zeros_like(acc)
    acc_far[...] = jnp.zeros_like(acc_far)

    def right_own(c, carry):
        cols = at(c * 512, 512)
        acc[...] += dot(ortho_st[:, cols], act[:, cols], NT)
        return carry

    lax.fori_loop(0, 8, right_own, 0)
    y_st[...] = stacked(folded(acc[...]))
    acc[...] = dot(y_st[...], grad[own, :])

    def right_error(c, carry):
        cols = at(c * 512, 512)
        acc[...] += dot(ortho_st[:, cols], error[cols, :])
        return carry

    lax.fori_loop(0, 8, right_error, 0)

    def merge_far(n, carry):
        cols = at(n * WIDE, WIDE)
        arrived(ACT + n, act_far.at[:, cols])
        piece = act_far[:, cols]
        merged[cols, :] += dot(piece, grad[far, :], TN)
        acc_far[...] += dot(ortho_st[:, cols], piece, NT)
        return carry

    lax.fori_loop(0, 12, merge_far, 0)
    plane_arrived(KZ, lambda n, py, pz: weight_far.at[left_cols(py, pz), :])
    send(KS, weight_far.at[my_half, :], weight_far.at[my_half, :], peer("S"))
    lax.fori_loop(12, PIECES, merge_far, 0)
    y_st[...] = stacked(folded(acc_far[...]))
    r0[...] = folded(acc[...] + dot(y_st[...], grad[far, :]))

    r_mine, r_other = at(core * 256, 256), at((1 - core) * 256, 256)
    send(RS, r0.at[:, r_other], r_sib, peer("S"))
    arrived(KS, weight_far.at[sib_half, :])
    arrived(RS, r_sib)
    r1[...] = r0[:, r_mine] + r_sib[...]

    def right_block(py, pz):
        return at(py * 16 + lax.div(pz, 2) * 8, 8), at(lax.rem(pz, 2) * 128, 128)

    plane_send(RZ, lambda py, pz: r1.at[right_block(py, pz)], lambda n: r_in.at[n])
    plane_arrived(RZ, lambda n, py, pz: r_in.at[n])

    def add_right(n, total):
        return total + r_in[n]

    r3[...] = lax.fori_loop(0, PEERS, add_right, r1[right_block(y, z)])
    send(RI, r3, r_i, peer("I"))
    send_kg(1)

    def store_grad(n, c):
        place = (kg_rows(n), at(c * 512, 512))
        return pltpu.make_async_copy(grad_stage.at[*place], input_grad.at[*place], store_sem.at[n])

    def input_far(n, c):
        rows, cols = kg_rows(n), at(c * 512, 512)
        term = dot(grad_far[rows, :], weight_far[cols, :], NT).astype(BF16)
        grad_stage[rows, cols] = (grad_stage[rows, cols].astype(F32) + term.astype(F32)).astype(BF16)
        store_grad(n, c).start()

    def input_first(c, carry):
        input_far(0, c)
        return carry

    def input_second(c, carry):
        input_far(1, c)
        return carry

    arrived(KG, grad_far.at[kg_rows(0), :])
    lax.fori_loop(0, 4, input_first, 0)
    arrived(RI, r_i)

    def full_block(py, pz):
        return (
            at(py * 16 + lax.div(pz, 2) * 8, 8),
            at(core * 256 + lax.rem(pz, 2) * 128, 128),
        )

    mine = full_block(y, z)
    right_full[mine] = (r3[...] + r_i[...]) * (1.0 / 64.0)
    plane_send(BZ, lambda py, pz: right_full.at[mine], lambda n: right_full.at[mine])
    lax.fori_loop(4, 8, input_first, 0)
    plane_arrived(BZ, lambda n, py, pz: right_full.at[full_block(py, pz)])
    send(BS, right_full.at[:, r_mine], right_full.at[:, r_mine], peer("S"))
    arrived(BS, right_full.at[:, r_other])
    right_out[...] = right_full[...]
    high, low = halves(right_full[...])
    right_fin[...] = jnp.concatenate((high, high, low, jnp.zeros_like(high)), axis=0)

    def store_error(n):
        rows = at(n * 256, 256)
        return pltpu.make_async_copy(err_stage.at[rows, :], error_out.at[rows, :], store_sem.at[2])

    def finish(n, carry):
        rows = at(n * 256, 256)
        err_stage[rows, :] = (merged[rows, :] - dot(ortho_nat[rows, :], right_fin[...])).astype(BF16)
        store_error(n).start()
        return carry

    lax.fori_loop(0, 16, finish, 0)
    arrived(KG + 1, grad_far.at[kg_rows(1), :])
    lax.fori_loop(0, 8, input_second, 0)

    for n in range(2):
        pltpu.make_async_copy(grad_stage.at[kg_rows(n), :], input_grad.at[kg_rows(n), :], store_sem.at[n]).wait()
    pltpu.make_async_copy(err_stage, error_out, store_sem.at[2]).wait()

    sources = {
        YSEND: y_own, KX: weight_in.at[k_rows, :], KS: weight_far.at[my_half, :],
        LS: left_part.at[:, sib_half], LX: left_z.at[:RANK], LX + 1: left_z.at[RANK:], LX + 2: left_z.at[RANK:],
        GS: left.at[:, my_half], RS: r0.at[:, r_other], RI: r3, BS: right_full.at[:, r_mine],
    }
    for n in range(PIECES):
        sources[ACT + n] = act_in.at[:, act_chunk(n)]
    for n in range(2):
        sources[KG + n] = grad_in.at[at(other * TOK + n * half_tok, half_tok), :]
    for n, src in sources.items():
        sent(n, src)
    plane_sent(KZ, lambda py, pz: weight_far.at[k_rows, :])
    plane_sent(LZ, lambda py, pz: left_half.at[:, plane_cols(py, pz)])
    plane_sent(GZ, lambda py, pz: left.at[:, col_z])
    plane_sent(RZ, lambda py, pz: r1.at[right_block(py, pz)])
    plane_sent(BZ, lambda py, pz: right_full.at[mine])


def shards(activations, key_grad, key_weight, error_prev, right_prev):
    def vmem(*shape, kind=F32):
        return pltpu.VMEM(shape, kind)

    input_grad, right_new, error_new = pl.pallas_call(
        kernel,
        out_shape=(
            jax.ShapeDtypeStruct((TOK, D), BF16),
            jax.ShapeDtypeStruct((RANK, COLS), F32),
            jax.ShapeDtypeStruct((D, COLS), BF16),
        ),
        in_specs=[pl.BlockSpec(memory_space=pl.ANY)] * 5,
        out_specs=(
            pl.BlockSpec(memory_space=pl.ANY),
            pl.BlockSpec(memory_space=pltpu.VMEM),
            pl.BlockSpec(memory_space=pl.ANY),
        ),
        scratch_shapes=[
            vmem(TOK, D, kind=BF16),
            vmem(TOK, D, kind=BF16),
            vmem(D, COLS, kind=BF16),
            vmem(2 * TOK, COLS, kind=BF16),
            vmem(TOK, COLS, kind=BF16),
            vmem(D, COLS, kind=BF16),
            vmem(D, COLS, kind=BF16),
            vmem(RANK, COLS),
            vmem(2 * RANK, COLS, kind=BF16),
            vmem(2 * RANK, TOK, kind=BF16),
            vmem(RANK, TOK),
            vmem(RANK, TOK),
            vmem(2 * RANK, D),
            vmem(2 * RANK, D // 2),
            vmem(2 * RANK, D // 2),
            vmem(PEERS, 2 * RANK, 128),
            vmem(2 * RANK, 128),
            vmem(3, RANK, 128),
            vmem(RANK, D),
            vmem(RANK, 2 * RANK),
            vmem(RANK, RANK),
            vmem(2 * RANK, D, kind=BF16),
            vmem(D, 4 * RANK, kind=BF16),
            vmem(D, COLS),
            vmem(D, COLS, kind=BF16),
            vmem(TOK, D, kind=BF16),
            vmem(2 * RANK, COLS),
            vmem(2 * RANK, TOK),
            vmem(RANK, COLS),
            vmem(RANK, 256),
            vmem(RANK, 256),
            vmem(PEERS, 8, 128),
            vmem(8, 128),
            vmem(8, 128),
            vmem(RANK, COLS),
            vmem(4 * RANK, COLS, kind=BF16),
            pltpu.SemaphoreType.DMA((5,)),
            pltpu.SemaphoreType.DMA((3,)),
            pltpu.SemaphoreType.DMA((N_COPIES,)),
            pltpu.SemaphoreType.DMA((N_COPIES,)),
        ],
        compiler_params=pltpu.CompilerParams(
            collective_id=0, has_side_effects=True, vmem_limit_bytes=60 * 2**20
        ),
    )(activations, key_grad, key_weight, error_prev, right_prev.T)
    return input_grad, right_new.T, error_new


def solution(mesh):
    placed = (
        P(("dp", "tensor"), None),
        P("dp", "tensor"),
        P(None, "tensor"),
        P("dp", "tensor"),
        P("tensor", None),
    )
    return jax.shard_map(
        shards,
        mesh=mesh,
        in_specs=placed,
        out_specs=(P(("dp", "tensor"), None), P("tensor", None), P("dp", "tensor")),
        check_vma=False,
    )
```

```python
import jax
import jax.numpy as jnp
from jax import lax
from jax.experimental import pallas as pl
from jax.experimental.pallas import tpu as pltpu
from jax.sharding import PartitionSpec as P

MESH = pl.DeviceIdType.MESH
HIGHEST = lax.Precision.HIGHEST
F32, BF16 = jnp.float32, jnp.bfloat16

TOK = 512
D = 4096
COLS = 512
RANK = 64
PIECES = 16
WIDE = D // PIECES
EARLY = 6

PEERS = 15
ACT = 0
YSEND = ACT + PIECES
KX, KZ, KS = YSEND + 1, YSEND + 2, YSEND + 2 + PEERS
LS, LZ, LX = KS + 1, KS + 2, KS + 2 + PEERS
GZ, GS = LX + 3, LX + 3 + PEERS
KG = GS + 1
RS, RZ, RI = KG + 2, KG + 3, KG + 3 + PEERS
BZ, BS = RI + 1, RI + 1 + PEERS
N_COPIES = BS + 1


def halves(value):
    high = value.astype(BF16)
    return high, (value - high.astype(F32)).astype(BF16)


def stacked(value):
    return jnp.concatenate(halves(value), axis=0)


def folded(value):
    half = value.shape[0] // 2
    return value[:half] + value[half:]


def dot(a, b, dims=((1,), (0,)), precision=None):
    return lax.dot_general(a, b, (dims, ((), ())), precision=precision, preferred_element_type=F32)


NT = ((1,), (1,))
TN = ((0,), (0,))


def kernel(
    act_in, grad_in, weight_in, error_in, right_in,
    right_out, merged_out, ortho_out, grad_out, grad_far, weight_out,
    act, act_far, error, grad, weight, weight_far, right,
    right_st, y_st, y_own, y_far, left_part, sib_in, left_half, plane_in, left_z, x_in,
    left, aug, low_inv, ortho_st, ortho_nat, merged, grad_stage, acc, acc_far,
    r0, r_sib, r1, r_in, r3, r_i, right_full,
    load_sem, store_sem, send_sem, recv_sem,
):
    dp, ten = lax.axis_index("dp"), lax.axis_index("tensor")
    z, y = lax.div(dp, 16), lax.rem(lax.div(dp, 4), 4)
    x_lo, core = lax.rem(lax.div(dp, 2), 2), lax.rem(dp, 2)
    other = 1 - ten

    def plane(k, sign=1):
        return lax.rem(y + sign * lax.div(k, 4) + 4, 4), lax.rem(z + sign * lax.rem(k, 4) + 4, 4)

    def peer(name, k=0):
        flipped = dp + 2 - 4 * x_lo
        if name == "S":
            return (dp + 1 - 2 * core, ten)
        if name == "I":
            return (flipped, ten)
        if name == "X":
            return (flipped, other)
        if name == "P":
            return (dp, other)
        py, pz = plane(k)
        return (dp + 4 * (py - y) + 16 * (pz - z), ten)

    def remote(n, src, dst, to):
        return pltpu.make_async_remote_copy(
            src_ref=src, dst_ref=dst, send_sem=send_sem.at[n], recv_sem=recv_sem.at[n],
            device_id=to, device_id_type=MESH,
        )

    def send(n, src, dst, to):
        remote(n, src, dst, to).start()

    def arrived(n, dst):
        remote(n, dst, dst, peer("P")).wait_recv()

    def sent(n, src):
        remote(n, src, src, peer("P")).wait_send()

    def plane_send(base, src, dst):
        def one(k, carry):
            send(base + k - 1, src(*plane(k)), dst(k - 1), peer("plane", k))
            return carry

        lax.fori_loop(1, PEERS + 1, one, 0)

    def plane_arrived(base, dst):
        def one(k, carry):
            arrived(base + k - 1, dst(k - 1, *plane(k, -1)))
            return carry

        lax.fori_loop(1, PEERS + 1, one, 0)

    def plane_sent(base, src):
        def one(k, carry):
            sent(base + k - 1, src(*plane(k)))
            return carry

        lax.fori_loop(1, PEERS + 1, one, 0)

    def at(start, size):
        return pl.ds(pl.multiple_of(start, size), size)

    stores = [
        pltpu.make_async_copy(src, dst, store_sem.at[n])
        for n, (src, dst) in enumerate(
            ((merged, merged_out), (grad_stage, grad_out), (ortho_nat, ortho_out), (weight_far, weight_out))
        )
    ]
    loads = [
        pltpu.make_async_copy(src, dst, load_sem.at[n])
        for n, (src, dst) in enumerate(
            ((right_in, right), (grad_in, grad), (act_in, act), (error_in, error), (weight_in, weight))
        )
    ]
    for load in loads:
        load.start()

    partners = [peer(name) for name in ("S", "I", "X", "P")]
    partners += [peer("plane", k) for k in range(1, PEERS + 1)]
    barrier = pltpu.get_barrier_semaphore()
    for to in partners:
        pl.semaphore_signal(barrier, inc=1, device_id=to, device_id_type=MESH)
    pl.semaphore_wait(barrier, len(partners))

    def act_chunk(n):
        return pl.ds(n * WIDE, WIDE)

    def send_act(n):
        send(ACT + n, act_in.at[:, act_chunk(n)], act_far.at[:, act_chunk(n)], peer("P"))

    k_rows = at(core * 2048 + y * 512 + z * 128, 128)
    send(KX, weight_in.at[k_rows, :], weight_far.at[k_rows, :], peer("P"))
    send_act(0)

    own, far = at(ten * TOK, TOK), at(other * TOK, TOK)
    loads[0].wait()
    loads[1].wait()
    right_st[...] = stacked(right[...])
    y_own[...] = folded(dot(right_st[...], grad[far, :], NT))
    send(YSEND, y_own, y_far, peer("P"))
    for n in range(1, EARLY):
        send_act(n)
    y_st[...] = stacked(folded(dot(right_st[...], grad[own, :], NT)))

    loads[2].wait()
    loads[3].wait()

    def left_own(c, carry):
        cols = at(c * 512, 512)
        part = dot(y_st[...], act[:, cols]) + dot(right_st[...], error[cols, :], NT)
        left_part[:RANK, cols] = folded(part)
        return carry

    lax.fori_loop(0, 8, left_own, 0)
    arrived(YSEND, y_far)
    y_st[...] = stacked(y_far[...])

    def left_other(c, carry):
        cols = at(c * 512, 512)
        left_part[RANK:, cols] = folded(dot(y_st[...], act[:, cols]))
        return carry

    lax.fori_loop(0, 8, left_other, 0)

    my_half, sib_half = at(core * 2048, 2048), at((1 - core) * 2048, 2048)
    send(LS, left_part.at[:, sib_half], sib_in, peer("S"))
    arrived(LS, sib_in)

    def add_sibling(c, carry):
        cols = at(c * 512, 512)
        left_half[:, cols] = left_part[:, at(core * 2048 + c * 512, 512)] + sib_in[:, cols]
        return carry

    lax.fori_loop(0, 4, add_sibling, 0)
    def plane_cols(py, pz):
        return at(py * 512 + pz * 128, 128)

    plane_send(LZ, lambda py, pz: left_half.at[:, plane_cols(py, pz)], lambda n: plane_in.at[n])

    def merge_own(n, carry):
        cols = at(n * WIDE, WIDE)
        merged[cols, :] = error[cols, :].astype(F32) + dot(act[:, cols], grad[own, :], TN)
        return carry

    lax.fori_loop(0, 12, merge_own, 0)
    plane_arrived(LZ, lambda n, py, pz: plane_in.at[n])

    def add_plane(n, total):
        return total + plane_in[n]

    left_z[...] = lax.fori_loop(0, PEERS, add_plane, left_half[:, plane_cols(y, z)])
    send(LX, left_z.at[:RANK], x_in.at[0], peer("I"))
    send(LX + 1, left_z.at[RANK:], x_in.at[1], peer("X"))
    send(LX + 2, left_z.at[RANK:], x_in.at[2], peer("P"))
    for n in range(EARLY, PIECES):
        send_act(n)
    half_tok = TOK // 2

    def kg_rows(n):
        return pl.ds(n * half_tok, half_tok)

    def send_kg(n):
        rows = at(other * TOK + n * half_tok, half_tok)
        send(KG + n, grad_in.at[rows, :], grad_far.at[kg_rows(n), :], peer("P"))

    send_kg(0)

    lax.fori_loop(12, 16, merge_own, 0)
    loads[4].wait()

    def input_own(c, carry):
        cols = at(c * 512, 512)
        grad_stage[:, cols] = dot(grad[own, :], weight[cols, :], NT).astype(BF16)
        return carry

    lax.fori_loop(0, 8, input_own, 0)
    stores[1].start()

    for k in range(3):
        arrived(LX + k, x_in.at[k])
    def left_cols(py, pz):
        return at(core * 2048 + py * 512 + pz * 128, 128)

    col_z = left_cols(y, z)
    left[:, col_z] = left_z[:RANK, :] + x_in[0] + x_in[1] + x_in[2]
    plane_send(GZ, lambda py, pz: left.at[:, col_z], lambda n: left.at[:, col_z])
    plane_arrived(GZ, lambda n, py, pz: left.at[:, left_cols(py, pz)])
    send(GS, left.at[:, my_half], left.at[:, my_half], peer("S"))
    arrived(KX, weight_far.at[k_rows, :])
    plane_send(KZ, lambda py, pz: weight_far.at[k_rows, :], lambda n: weight_far.at[k_rows, :])
    arrived(GS, left.at[:, sib_half])

    def gram_step(c, total):
        part = left[:, at(c * 512, 512)]
        return total + dot(part, part, NT, HIGHEST)

    aug[:, :RANK] = lax.fori_loop(0, 8, gram_step, jnp.zeros((RANK, RANK), F32))
    sub = lax.broadcasted_iota(jnp.int32, (RANK, 2 * RANK), 0)
    lane = lax.broadcasted_iota(jnp.int32, (RANK, 2 * RANK), 1)
    aug[:, RANK:] = (sub == lane).astype(F32)[:, :RANK]

    def eliminate(j, carry):
        mat, pivots = carry
        row = jnp.sum(jnp.where(sub == j, mat, 0.0), axis=0, keepdims=True)
        col = jnp.sum(jnp.where(lane == j, mat, 0.0), axis=1, keepdims=True)
        pivot = jnp.sum(jnp.where(lane[:1] == j, row, 0.0), axis=1, keepdims=True)
        pivots = jnp.where(sub == j, pivot, pivots)
        factor = jnp.where(sub > j, col / pivot, 0.0)
        return mat - factor * row, pivots

    mat, pivots = lax.fori_loop(0, RANK, eliminate, (aug[...], jnp.ones((RANK, 2 * RANK), F32)))
    aug[...] = mat / jnp.sqrt(pivots)
    low_inv[...] = aug[:, RANK:]

    def ortho_step(c, carry):
        cols = at(c * 512, 512)
        high, low = halves(dot(low_inv[...], left[:, cols], precision=HIGHEST))
        ortho_st[:RANK, cols] = high
        ortho_st[RANK:, cols] = low
        ortho_nat[cols, :] = jnp.concatenate((high, low), axis=0).T
        return carry

    lax.fori_loop(0, 8, ortho_step, 0)
    stores[2].start()

    acc[...] = jnp.zeros_like(acc)
    acc_far[...] = jnp.zeros_like(acc_far)

    def right_own(c, carry):
        cols = at(c * 512, 512)
        acc[...] += dot(ortho_st[:, cols], act[:, cols], NT)
        return carry

    lax.fori_loop(0, 8, right_own, 0)
    y_st[...] = stacked(folded(acc[...]))
    acc[...] = dot(y_st[...], grad[own, :])

    def right_error(c, carry):
        cols = at(c * 512, 512)
        acc[...] += dot(ortho_st[:, cols], error[cols, :])
        return carry

    lax.fori_loop(0, 8, right_error, 0)

    def merge_far(n, carry):
        cols = at(n * WIDE, WIDE)
        arrived(ACT + n, act_far.at[:, cols])
        piece = act_far[:, cols]
        merged[cols, :] += dot(piece, grad[far, :], TN)
        pltpu.make_async_copy(merged.at[cols, :], merged_out.at[cols, :], store_sem.at[0]).start()
        acc_far[...] += dot(ortho_st[:, cols], piece, NT)
        return carry

    lax.fori_loop(0, 12, merge_far, 0)
    plane_arrived(KZ, lambda n, py, pz: weight_far.at[left_cols(py, pz), :])
    send(KS, weight_far.at[my_half, :], weight_far.at[my_half, :], peer("S"))
    lax.fori_loop(12, PIECES, merge_far, 0)
    y_st[...] = stacked(folded(acc_far[...]))
    r0[...] = folded(acc[...] + dot(y_st[...], grad[far, :]))

    r_mine, r_other = at(core * 256, 256), at((1 - core) * 256, 256)
    send(RS, r0.at[:, r_other], r_sib, peer("S"))
    arrived(KS, weight_far.at[sib_half, :])
    stores[3].start()
    arrived(RS, r_sib)
    r1[...] = r0[:, r_mine] + r_sib[...]

    def right_block(py, pz):
        return at(py * 16 + lax.div(pz, 2) * 8, 8), at(lax.rem(pz, 2) * 128, 128)

    plane_send(RZ, lambda py, pz: r1.at[right_block(py, pz)], lambda n: r_in.at[n])
    plane_arrived(RZ, lambda n, py, pz: r_in.at[n])

    def add_right(n, total):
        return total + r_in[n]

    r3[...] = lax.fori_loop(0, PEERS, add_right, r1[right_block(y, z)])
    send(RI, r3, r_i, peer("I"))
    send_kg(1)

    arrived(RI, r_i)

    def full_block(py, pz):
        return (
            at(py * 16 + lax.div(pz, 2) * 8, 8),
            at(core * 256 + lax.rem(pz, 2) * 128, 128),
        )

    mine = full_block(y, z)
    right_full[mine] = (r3[...] + r_i[...]) * (1.0 / 64.0)
    plane_send(BZ, lambda py, pz: right_full.at[mine], lambda n: right_full.at[mine])
    plane_arrived(BZ, lambda n, py, pz: right_full.at[full_block(py, pz)])
    send(BS, right_full.at[:, r_mine], right_full.at[:, r_mine], peer("S"))
    arrived(BS, right_full.at[:, r_other])
    right_out[...] = right_full[...]
    for n in range(2):
        arrived(KG + n, grad_far.at[kg_rows(n), :])
    for store in stores:
        store.wait()

    sources = {
        YSEND: y_own, KX: weight_in.at[k_rows, :], KS: weight_far.at[my_half, :],
        LS: left_part.at[:, sib_half], LX: left_z.at[:RANK], LX + 1: left_z.at[RANK:], LX + 2: left_z.at[RANK:],
        GS: left.at[:, my_half], RS: r0.at[:, r_other], RI: r3, BS: right_full.at[:, r_mine],
    }
    for n in range(PIECES):
        sources[ACT + n] = act_in.at[:, act_chunk(n)]
    for n in range(2):
        sources[KG + n] = grad_in.at[at(other * TOK + n * half_tok, half_tok), :]
    for n, src in sources.items():
        sent(n, src)
    plane_sent(KZ, lambda py, pz: weight_far.at[k_rows, :])
    plane_sent(LZ, lambda py, pz: left_half.at[:, plane_cols(py, pz)])
    plane_sent(GZ, lambda py, pz: left.at[:, col_z])
    plane_sent(RZ, lambda py, pz: r1.at[right_block(py, pz)])
    plane_sent(BZ, lambda py, pz: right_full.at[mine])


def finish(merged, ortho, right, grad_own, weight_far, grad_far, input_grad, right_new, error_new):
    high, low = halves(right[...])
    approx = dot(ortho[...], jnp.concatenate((high, high), axis=0)) + dot(ortho[:, :RANK], low)
    error_new[...] = (merged[...] - approx).astype(BF16)
    term = dot(grad_far[...], weight_far[...], NT).astype(BF16)
    input_grad[...] = (grad_own[...].astype(F32) + term.astype(F32)).astype(BF16)
    right_new[...] = right[...]


def shards(activations, key_grad, key_weight, error_prev, right_prev):
    def vmem(*shape, kind=F32):
        return pltpu.VMEM(shape, kind)

    def array(*shape, kind=BF16):
        return jax.ShapeDtypeStruct(shape, kind)

    anywhere = pl.BlockSpec(memory_space=pl.ANY)
    right, merged, ortho, grad_own, grad_far, weight_far = pl.pallas_call(
        kernel,
        out_shape=(
            array(RANK, COLS, kind=F32),
            array(D, COLS, kind=F32),
            array(D, 2 * RANK),
            array(TOK, D),
            array(TOK, COLS),
            array(D, COLS),
        ),
        in_specs=[anywhere] * 5,
        out_specs=(pl.BlockSpec(memory_space=pltpu.VMEM),) + (anywhere,) * 5,
        scratch_shapes=[
            vmem(TOK, D, kind=BF16),
            vmem(TOK, D, kind=BF16),
            vmem(D, COLS, kind=BF16),
            vmem(2 * TOK, COLS, kind=BF16),
            vmem(D, COLS, kind=BF16),
            vmem(D, COLS, kind=BF16),
            vmem(RANK, COLS),
            vmem(2 * RANK, COLS, kind=BF16),
            vmem(2 * RANK, TOK, kind=BF16),
            vmem(RANK, TOK),
            vmem(RANK, TOK),
            vmem(2 * RANK, D),
            vmem(2 * RANK, D // 2),
            vmem(2 * RANK, D // 2),
            vmem(PEERS, 2 * RANK, 128),
            vmem(2 * RANK, 128),
            vmem(3, RANK, 128),
            vmem(RANK, D),
            vmem(RANK, 2 * RANK),
            vmem(RANK, RANK),
            vmem(2 * RANK, D, kind=BF16),
            vmem(D, 2 * RANK, kind=BF16),
            vmem(D, COLS),
            vmem(TOK, D, kind=BF16),
            vmem(2 * RANK, COLS),
            vmem(2 * RANK, TOK),
            vmem(RANK, COLS),
            vmem(RANK, 256),
            vmem(RANK, 256),
            vmem(PEERS, 8, 128),
            vmem(8, 128),
            vmem(8, 128),
            vmem(RANK, COLS),
            pltpu.SemaphoreType.DMA((5,)),
            pltpu.SemaphoreType.DMA((4,)),
            pltpu.SemaphoreType.DMA((N_COPIES,)),
            pltpu.SemaphoreType.DMA((N_COPIES,)),
        ],
        compiler_params=pltpu.CompilerParams(
            collective_id=0, has_side_effects=True, vmem_limit_bytes=60 * 2**20
        ),
    )(activations, key_grad, key_weight, error_prev, right_prev.T)
    steps = 8
    rows, cols = D // steps, D // steps

    def whole(*shape):
        return pl.BlockSpec(shape, lambda i: (0, 0))

    def down(*shape):
        return pl.BlockSpec(shape, lambda i: (i, 0))

    def along(*shape):
        return pl.BlockSpec(shape, lambda i: (0, i))

    input_grad, right_new, error_new = pl.pallas_call(
        finish,
        grid=(steps,),
        out_shape=(array(TOK, D), array(RANK, COLS, kind=F32), array(D, COLS)),
        in_specs=[
            down(rows, COLS), down(rows, 2 * RANK), whole(RANK, COLS),
            along(TOK, cols), down(cols, COLS), whole(TOK, COLS),
        ],
        out_specs=(along(TOK, cols), whole(RANK, COLS), down(rows, COLS)),
        compiler_params=pltpu.CompilerParams(vmem_limit_bytes=60 * 2**20),
    )(merged, ortho, right, grad_own, weight_far, grad_far)
    return input_grad, right_new.T, error_new


def solution(mesh):
    placed = (
        P(("dp", "tensor"), None),
        P("dp", "tensor"),
        P(None, "tensor"),
        P("dp", "tensor"),
        P("tensor", None),
    )
    return jax.shard_map(
        shards,
        mesh=mesh,
        in_specs=placed,
        out_specs=(P(("dp", "tensor"), None), P("tensor", None), P("dp", "tensor")),
        check_vma=False,
    )
```

```python
import jax
import jax.numpy as jnp
from jax import lax
from jax.experimental import pallas as pl
from jax.experimental.pallas import tpu as pltpu
from jax.sharding import PartitionSpec as P

MESH = pl.DeviceIdType.MESH
HIGHEST = lax.Precision.HIGHEST
F32, BF16 = jnp.float32, jnp.bfloat16

TOK = 512
D = 4096
COLS = 512
RANK = 64
PIECES = 16
WIDE = D // PIECES
FINAL = 512
EARLY = 6

PEERS = 15
ACT = 0
YSEND = ACT + PIECES
KX, KZ, KS = YSEND + 1, YSEND + 2, YSEND + 2 + PEERS
LS, LZ, LX = KS + 1, KS + 2, KS + 2 + PEERS
GZ, GS = LX + 3, LX + 3 + PEERS
KG = GS + 1
RS, RZ, RI = KG + 2, KG + 3, KG + 3 + PEERS
BZ, BS = RI + 1, RI + 1 + PEERS
N_COPIES = BS + 1


def halves(value):
    high = value.astype(BF16)
    return high, (value - high.astype(F32)).astype(BF16)


def stacked(value):
    return jnp.concatenate(halves(value), axis=0)


def folded(value):
    half = value.shape[0] // 2
    return value[:half] + value[half:]


def dot(a, b, dims=((1,), (0,)), precision=None):
    return lax.dot_general(a, b, (dims, ((), ())), precision=precision, preferred_element_type=F32)


NT = ((1,), (1,))
TN = ((0,), (0,))


def kernel(
    act_in, grad_in, weight_in, error_in, right_in,
    right_out, merged_out, ortho_out, grad_out, grad_far, weight_out,
    act, act_far, error, grad, weight, weight_far, right,
    right_st, y_st, y_own, y_far, left_part, sib_in, left_half, plane_in, left_z, x_in,
    left, aug, low_inv, ortho_st, ortho_nat, merged, grad_stage, acc, acc_far,
    r0, r_sib, r1, r_in, r3, r_i, right_full,
    load_sem, store_sem, send_sem, recv_sem,
):
    dp, ten = lax.axis_index("dp"), lax.axis_index("tensor")
    z, y = lax.div(dp, 16), lax.rem(lax.div(dp, 4), 4)
    x_lo, core = lax.rem(lax.div(dp, 2), 2), lax.rem(dp, 2)
    other = 1 - ten

    def plane(k, sign=1):
        return lax.rem(y + sign * lax.div(k, 4) + 4, 4), lax.rem(z + sign * lax.rem(k, 4) + 4, 4)

    def peer(name, k=0):
        flipped = dp + 2 - 4 * x_lo
        if name == "S":
            return (dp + 1 - 2 * core, ten)
        if name == "I":
            return (flipped, ten)
        if name == "X":
            return (flipped, other)
        if name == "P":
            return (dp, other)
        py, pz = plane(k)
        return (dp + 4 * (py - y) + 16 * (pz - z), ten)

    def remote(n, src, dst, to):
        return pltpu.make_async_remote_copy(
            src_ref=src, dst_ref=dst, send_sem=send_sem.at[n], recv_sem=recv_sem.at[n],
            device_id=to, device_id_type=MESH,
        )

    def send(n, src, dst, to):
        remote(n, src, dst, to).start()

    def arrived(n, dst):
        remote(n, dst, dst, peer("P")).wait_recv()

    def sent(n, src):
        remote(n, src, src, peer("P")).wait_send()

    def plane_send(base, src, dst):
        def one(k, carry):
            send(base + k - 1, src(*plane(k)), dst(k - 1), peer("plane", k))
            return carry

        lax.fori_loop(1, PEERS + 1, one, 0)

    def plane_arrived(base, dst):
        def one(k, carry):
            arrived(base + k - 1, dst(k - 1, *plane(k, -1)))
            return carry

        lax.fori_loop(1, PEERS + 1, one, 0)

    def plane_sent(base, src):
        def one(k, carry):
            sent(base + k - 1, src(*plane(k)))
            return carry

        lax.fori_loop(1, PEERS + 1, one, 0)

    def at(start, size):
        return pl.ds(pl.multiple_of(start, size), size)

    stores = [
        pltpu.make_async_copy(src, dst, store_sem.at[n])
        for n, (src, dst) in enumerate(
            ((merged, merged_out), (grad_stage, grad_out), (ortho_nat, ortho_out), (weight_far, weight_out))
        )
    ]
    loads = [
        pltpu.make_async_copy(src, dst, load_sem.at[n])
        for n, (src, dst) in enumerate(
            ((right_in, right), (grad_in, grad), (act_in, act), (error_in, error), (weight_in, weight))
        )
    ]
    for load in loads:
        load.start()

    partners = [peer(name) for name in ("S", "I", "X", "P")]
    partners += [peer("plane", k) for k in range(1, PEERS + 1)]
    barrier = pltpu.get_barrier_semaphore()
    for to in partners:
        pl.semaphore_signal(barrier, inc=1, device_id=to, device_id_type=MESH)
    pl.semaphore_wait(barrier, len(partners))

    def act_chunk(n):
        return pl.ds(n * WIDE, WIDE)

    def send_act(n):
        send(ACT + n, act_in.at[:, act_chunk(n)], act_far.at[:, act_chunk(n)], peer("P"))

    k_rows = at(core * 2048 + y * 512 + z * 128, 128)
    send(KX, weight_in.at[k_rows, :], weight_far.at[k_rows, :], peer("P"))
    send_act(0)

    own, far = at(ten * TOK, TOK), at(other * TOK, TOK)
    loads[0].wait()
    loads[1].wait()
    right_st[...] = stacked(right[...])
    y_own[...] = folded(dot(right_st[...], grad[far, :], NT))
    send(YSEND, y_own, y_far, peer("P"))
    for n in range(1, EARLY):
        send_act(n)
    y_st[...] = stacked(folded(dot(right_st[...], grad[own, :], NT)))

    loads[2].wait()
    loads[3].wait()

    def left_own(c, carry):
        cols = at(c * 512, 512)
        part = dot(y_st[...], act[:, cols]) + dot(right_st[...], error[cols, :], NT)
        left_part[:RANK, cols] = folded(part)
        return carry

    lax.fori_loop(0, 8, left_own, 0)
    arrived(YSEND, y_far)
    y_st[...] = stacked(y_far[...])

    def left_other(c, carry):
        cols = at(c * 512, 512)
        left_part[RANK:, cols] = folded(dot(y_st[...], act[:, cols]))
        return carry

    lax.fori_loop(0, 8, left_other, 0)

    my_half, sib_half = at(core * 2048, 2048), at((1 - core) * 2048, 2048)
    send(LS, left_part.at[:, sib_half], sib_in, peer("S"))
    arrived(LS, sib_in)

    def add_sibling(c, carry):
        cols = at(c * 512, 512)
        left_half[:, cols] = left_part[:, at(core * 2048 + c * 512, 512)] + sib_in[:, cols]
        return carry

    lax.fori_loop(0, 4, add_sibling, 0)
    def plane_cols(py, pz):
        return at(py * 512 + pz * 128, 128)

    plane_send(LZ, lambda py, pz: left_half.at[:, plane_cols(py, pz)], lambda n: plane_in.at[n])

    def merge_own(n, carry):
        cols = at(n * WIDE, WIDE)
        merged[cols, :] = error[cols, :].astype(F32) + dot(act[:, cols], grad[own, :], TN)
        return carry

    lax.fori_loop(0, 12, merge_own, 0)
    plane_arrived(LZ, lambda n, py, pz: plane_in.at[n])

    def add_plane(n, total):
        return total + plane_in[n]

    left_z[...] = lax.fori_loop(0, PEERS, add_plane, left_half[:, plane_cols(y, z)])
    send(LX, left_z.at[:RANK], x_in.at[0], peer("I"))
    send(LX + 1, left_z.at[RANK:], x_in.at[1], peer("X"))
    send(LX + 2, left_z.at[RANK:], x_in.at[2], peer("P"))
    for n in range(EARLY, PIECES):
        send_act(n)
    half_tok = TOK // 2

    def kg_rows(n):
        return pl.ds(n * half_tok, half_tok)

    def send_kg(n):
        rows = at(other * TOK + n * half_tok, half_tok)
        send(KG + n, grad_in.at[rows, :], grad_far.at[kg_rows(n), :], peer("P"))

    send_kg(0)

    lax.fori_loop(12, 16, merge_own, 0)
    loads[4].wait()

    def input_own(c, carry):
        cols = at(c * 512, 512)
        grad_stage[:, cols] = dot(grad[own, :], weight[cols, :], NT).astype(BF16)
        return carry

    lax.fori_loop(0, 8, input_own, 0)
    stores[1].start()

    for k in range(3):
        arrived(LX + k, x_in.at[k])
    def left_cols(py, pz):
        return at(core * 2048 + py * 512 + pz * 128, 128)

    col_z = left_cols(y, z)
    left[:, col_z] = left_z[:RANK, :] + x_in[0] + x_in[1] + x_in[2]
    plane_send(GZ, lambda py, pz: left.at[:, col_z], lambda n: left.at[:, col_z])
    plane_arrived(GZ, lambda n, py, pz: left.at[:, left_cols(py, pz)])
    send(GS, left.at[:, my_half], left.at[:, my_half], peer("S"))
    arrived(KX, weight_far.at[k_rows, :])
    plane_send(KZ, lambda py, pz: weight_far.at[k_rows, :], lambda n: weight_far.at[k_rows, :])
    arrived(GS, left.at[:, sib_half])

    def gram_step(c, total):
        part = left[:, at(c * 512, 512)]
        return total + dot(part, part, NT, HIGHEST)

    aug[:, :RANK] = lax.fori_loop(0, 8, gram_step, jnp.zeros((RANK, RANK), F32))
    sub = lax.broadcasted_iota(jnp.int32, (RANK, 2 * RANK), 0)
    lane = lax.broadcasted_iota(jnp.int32, (RANK, 2 * RANK), 1)
    aug[:, RANK:] = (sub == lane).astype(F32)[:, :RANK]

    def eliminate(j, carry):
        mat, pivots = carry
        row = jnp.sum(jnp.where(sub == j, mat, 0.0), axis=0, keepdims=True)
        col = jnp.sum(jnp.where(lane == j, mat, 0.0), axis=1, keepdims=True)
        pivot = jnp.sum(jnp.where(lane[:1] == j, row, 0.0), axis=1, keepdims=True)
        pivots = jnp.where(sub == j, pivot, pivots)
        factor = jnp.where(sub > j, col / pivot, 0.0)
        return mat - factor * row, pivots

    mat, pivots = lax.fori_loop(0, RANK, eliminate, (aug[...], jnp.ones((RANK, 2 * RANK), F32)))
    aug[...] = mat / jnp.sqrt(pivots)
    low_inv[...] = aug[:, RANK:]

    def ortho_step(c, carry):
        cols = at(c * 512, 512)
        high, low = halves(dot(low_inv[...], left[:, cols], precision=HIGHEST))
        ortho_st[:RANK, cols] = high
        ortho_st[RANK:, cols] = low
        ortho_nat[cols, :] = jnp.concatenate((high, low), axis=0).T
        return carry

    lax.fori_loop(0, 8, ortho_step, 0)
    stores[2].start()

    acc[...] = jnp.zeros_like(acc)
    acc_far[...] = jnp.zeros_like(acc_far)

    def right_own(c, carry):
        cols = at(c * 512, 512)
        acc[...] += dot(ortho_st[:, cols], act[:, cols], NT)
        return carry

    lax.fori_loop(0, 8, right_own, 0)
    y_st[...] = stacked(folded(acc[...]))
    acc[...] = dot(y_st[...], grad[own, :])

    def right_error(c, carry):
        cols = at(c * 512, 512)
        acc[...] += dot(ortho_st[:, cols], error[cols, :])
        return carry

    lax.fori_loop(0, 8, right_error, 0)

    def merge_far(n, carry):
        cols = at(n * WIDE, WIDE)
        arrived(ACT + n, act_far.at[:, cols])
        piece = act_far[:, cols]
        merged[cols, :] += dot(piece, grad[far, :], TN)
        pltpu.make_async_copy(merged.at[cols, :], merged_out.at[cols, :], store_sem.at[0]).start()
        acc_far[...] += dot(ortho_st[:, cols], piece, NT)
        return carry

    lax.fori_loop(0, 12, merge_far, 0)
    plane_arrived(KZ, lambda n, py, pz: weight_far.at[left_cols(py, pz), :])
    send(KS, weight_far.at[my_half, :], weight_far.at[my_half, :], peer("S"))
    lax.fori_loop(12, PIECES, merge_far, 0)
    y_st[...] = stacked(folded(acc_far[...]))
    r0[...] = folded(acc[...] + dot(y_st[...], grad[far, :]))

    r_mine, r_other = at(core * 256, 256), at((1 - core) * 256, 256)
    send(RS, r0.at[:, r_other], r_sib, peer("S"))
    arrived(KS, weight_far.at[sib_half, :])
    stores[3].start()
    arrived(RS, r_sib)
    r1[...] = r0[:, r_mine] + r_sib[...]

    def right_block(py, pz):
        return at(py * 16 + lax.div(pz, 2) * 8, 8), at(lax.rem(pz, 2) * 128, 128)

    plane_send(RZ, lambda py, pz: r1.at[right_block(py, pz)], lambda n: r_in.at[n])
    plane_arrived(RZ, lambda n, py, pz: r_in.at[n])

    def add_right(n, total):
        return total + r_in[n]

    r3[...] = lax.fori_loop(0, PEERS, add_right, r1[right_block(y, z)])
    send(RI, r3, r_i, peer("I"))
    send_kg(1)

    arrived(RI, r_i)

    def full_block(py, pz):
        return (
            at(py * 16 + lax.div(pz, 2) * 8, 8),
            at(core * 256 + lax.rem(pz, 2) * 128, 128),
        )

    mine = full_block(y, z)
    right_full[mine] = (r3[...] + r_i[...]) * (1.0 / 64.0)
    plane_send(BZ, lambda py, pz: right_full.at[mine], lambda n: right_full.at[mine])
    plane_arrived(BZ, lambda n, py, pz: right_full.at[full_block(py, pz)])
    send(BS, right_full.at[:, r_mine], right_full.at[:, r_mine], peer("S"))
    arrived(BS, right_full.at[:, r_other])
    right_out[...] = right_full[...]
    for n in range(2):
        arrived(KG + n, grad_far.at[kg_rows(n), :])
    for store in stores:
        store.wait()

    sources = {
        YSEND: y_own, KX: weight_in.at[k_rows, :], KS: weight_far.at[my_half, :],
        LS: left_part.at[:, sib_half], LX: left_z.at[:RANK], LX + 1: left_z.at[RANK:], LX + 2: left_z.at[RANK:],
        GS: left.at[:, my_half], RS: r0.at[:, r_other], RI: r3, BS: right_full.at[:, r_mine],
    }
    for n in range(PIECES):
        sources[ACT + n] = act_in.at[:, act_chunk(n)]
    for n in range(2):
        sources[KG + n] = grad_in.at[at(other * TOK + n * half_tok, half_tok), :]
    for n, src in sources.items():
        sent(n, src)
    plane_sent(KZ, lambda py, pz: weight_far.at[k_rows, :])
    plane_sent(LZ, lambda py, pz: left_half.at[:, plane_cols(py, pz)])
    plane_sent(GZ, lambda py, pz: left.at[:, col_z])
    plane_sent(RZ, lambda py, pz: r1.at[right_block(py, pz)])
    plane_sent(BZ, lambda py, pz: right_full.at[mine])


def finish(
    merged_in, ortho_in, right, own_in, weight_in, grad_in,
    input_grad, right_new, error_new,
    merged, ortho, own, weight, grad, error, grad_sem, load_sem, store_sem,
):
    load_grad = pltpu.make_async_copy(grad_in, grad, grad_sem)
    load_grad.start()

    def span(n):
        return pl.ds(n * FINAL, FINAL)

    def loads(n):
        pairs = (
            (weight_in.at[span(n), :], weight.at[span(n), :]),
            (own_in.at[:, span(n)], own.at[:, span(n)]),
            (ortho_in.at[span(n), :], ortho.at[span(n), :]),
            (merged_in.at[span(n), :], merged.at[span(n), :]),
        )
        return [pltpu.make_async_copy(src, dst, load_sem.at[n, k]) for k, (src, dst) in enumerate(pairs)]

    for n in range(D // FINAL):
        for load in loads(n):
            load.start()
    high, low = halves(right[...])
    twice = jnp.concatenate((high, high), axis=0)
    right_new[...] = right[...]
    load_grad.wait()
    for n in range(D // FINAL):
        for load in loads(n):
            load.wait()
        term = dot(grad[...], weight[span(n), :], NT).astype(BF16)
        own[:, span(n)] = (own[:, span(n)].astype(F32) + term.astype(F32)).astype(BF16)
        pltpu.make_async_copy(own.at[:, span(n)], input_grad.at[:, span(n)], store_sem.at[0]).start()
        approx = dot(ortho[span(n), :], twice) + dot(ortho[span(n), :RANK], low)
        error[span(n), :] = (merged[span(n), :] - approx).astype(BF16)
        pltpu.make_async_copy(error.at[span(n), :], error_new.at[span(n), :], store_sem.at[1]).start()
    pltpu.make_async_copy(own, input_grad, store_sem.at[0]).wait()
    pltpu.make_async_copy(error, error_new, store_sem.at[1]).wait()


def shards(activations, key_grad, key_weight, error_prev, right_prev):
    def vmem(*shape, kind=F32):
        return pltpu.VMEM(shape, kind)

    def array(*shape, kind=BF16):
        return jax.ShapeDtypeStruct(shape, kind)

    anywhere = pl.BlockSpec(memory_space=pl.ANY)
    in_vmem = pl.BlockSpec(memory_space=pltpu.VMEM)
    right, merged, ortho, grad_own, grad_far, weight_far = pl.pallas_call(
        kernel,
        out_shape=(
            array(RANK, COLS, kind=F32),
            array(D, COLS, kind=F32),
            array(D, 2 * RANK),
            array(TOK, D),
            array(TOK, COLS),
            array(D, COLS),
        ),
        in_specs=[anywhere] * 5,
        out_specs=(in_vmem,) + (anywhere,) * 5,
        scratch_shapes=[
            vmem(TOK, D, kind=BF16),
            vmem(TOK, D, kind=BF16),
            vmem(D, COLS, kind=BF16),
            vmem(2 * TOK, COLS, kind=BF16),
            vmem(D, COLS, kind=BF16),
            vmem(D, COLS, kind=BF16),
            vmem(RANK, COLS),
            vmem(2 * RANK, COLS, kind=BF16),
            vmem(2 * RANK, TOK, kind=BF16),
            vmem(RANK, TOK),
            vmem(RANK, TOK),
            vmem(2 * RANK, D),
            vmem(2 * RANK, D // 2),
            vmem(2 * RANK, D // 2),
            vmem(PEERS, 2 * RANK, 128),
            vmem(2 * RANK, 128),
            vmem(3, RANK, 128),
            vmem(RANK, D),
            vmem(RANK, 2 * RANK),
            vmem(RANK, RANK),
            vmem(2 * RANK, D, kind=BF16),
            vmem(D, 2 * RANK, kind=BF16),
            vmem(D, COLS),
            vmem(TOK, D, kind=BF16),
            vmem(2 * RANK, COLS),
            vmem(2 * RANK, TOK),
            vmem(RANK, COLS),
            vmem(RANK, 256),
            vmem(RANK, 256),
            vmem(PEERS, 8, 128),
            vmem(8, 128),
            vmem(8, 128),
            vmem(RANK, COLS),
            pltpu.SemaphoreType.DMA((5,)),
            pltpu.SemaphoreType.DMA((4,)),
            pltpu.SemaphoreType.DMA((N_COPIES,)),
            pltpu.SemaphoreType.DMA((N_COPIES,)),
        ],
        compiler_params=pltpu.CompilerParams(
            collective_id=0, has_side_effects=True, vmem_limit_bytes=60 * 2**20
        ),
    )(activations, key_grad, key_weight, error_prev, right_prev.T)
    input_grad, right_new, error_new = pl.pallas_call(
        finish,
        out_shape=(array(TOK, D), array(RANK, COLS, kind=F32), array(D, COLS)),
        in_specs=[anywhere, anywhere, in_vmem, anywhere, anywhere, anywhere],
        out_specs=(anywhere, in_vmem, anywhere),
        scratch_shapes=[
            vmem(D, COLS),
            vmem(D, 2 * RANK, kind=BF16),
            vmem(TOK, D, kind=BF16),
            vmem(D, COLS, kind=BF16),
            vmem(TOK, COLS, kind=BF16),
            vmem(D, COLS, kind=BF16),
            pltpu.SemaphoreType.DMA,
            pltpu.SemaphoreType.DMA((D // FINAL, 4)),
            pltpu.SemaphoreType.DMA((2,)),
        ],
        compiler_params=pltpu.CompilerParams(vmem_limit_bytes=60 * 2**20),
    )(merged, ortho, right, grad_own, weight_far, grad_far)
    return input_grad, right_new.T, error_new


def solution(mesh):
    placed = (
        P(("dp", "tensor"), None),
        P("dp", "tensor"),
        P(None, "tensor"),
        P("dp", "tensor"),
        P("tensor", None),
    )
    return jax.shard_map(
        shards,
        mesh=mesh,
        in_specs=placed,
        out_specs=(P(("dp", "tensor"), None), P("tensor", None), P("dp", "tensor")),
        check_vma=False,
    )
```

```python
import jax
import jax.numpy as jnp
from jax import lax
from jax.experimental import pallas as pl
from jax.experimental.pallas import tpu as pltpu
from jax.sharding import PartitionSpec as P

MESH = pl.DeviceIdType.MESH
HIGHEST = lax.Precision.HIGHEST
F32, BF16 = jnp.float32, jnp.bfloat16

TOK = 512
D = 4096
COLS = 512
RANK = 64
PIECES = 16
WIDE = D // PIECES
EARLY = 6

PEERS = 15
ACT = 0
YSEND = ACT + PIECES
KX, KZ, KS = YSEND + 1, YSEND + 2, YSEND + 2 + PEERS
LS, LZ, LX = KS + 1, KS + 2, KS + 2 + PEERS
GZ, GS = LX + 3, LX + 3 + PEERS
KG = GS + 1
RS, RZ, RI = KG + 2, KG + 3, KG + 3 + PEERS
BZ, BS = RI + 1, RI + 1 + PEERS
N_COPIES = BS + 1


def halves(value):
    high = value.astype(BF16)
    return high, (value - high.astype(F32)).astype(BF16)


def stacked(value):
    return jnp.concatenate(halves(value), axis=0)


def folded(value):
    half = value.shape[0] // 2
    return value[:half] + value[half:]


def dot(a, b, dims=((1,), (0,)), precision=None):
    return lax.dot_general(a, b, (dims, ((), ())), precision=precision, preferred_element_type=F32)


NT = ((1,), (1,))
TN = ((0,), (0,))


def kernel(
    act_in, grad_in, weight_in, error_in, right_in,
    right_out, merged_out, ortho_out, grad_out, grad_far, weight_out,
    act, act_far, error, grad, weight, weight_far, right,
    right_st, y_st, y_own, y_far, left_part, sib_in, left_half, plane_in, left_z, x_in,
    left, aug, low_inv, ortho_st, ortho_nat, merged, grad_stage, acc, acc_far,
    r0, r_sib, r1, r_in, r3, r_i, right_full,
    load_sem, store_sem, send_sem, recv_sem,
):
    dp, ten = lax.axis_index("dp"), lax.axis_index("tensor")
    z, y = lax.div(dp, 16), lax.rem(lax.div(dp, 4), 4)
    x_lo, core = lax.rem(lax.div(dp, 2), 2), lax.rem(dp, 2)
    other = 1 - ten

    def plane(k, sign=1):
        return lax.rem(y + sign * lax.div(k, 4) + 4, 4), lax.rem(z + sign * lax.rem(k, 4) + 4, 4)

    def peer(name, k=0):
        flipped = dp + 2 - 4 * x_lo
        if name == "S":
            return (dp + 1 - 2 * core, ten)
        if name == "I":
            return (flipped, ten)
        if name == "X":
            return (flipped, other)
        if name == "P":
            return (dp, other)
        py, pz = plane(k)
        return (dp + 4 * (py - y) + 16 * (pz - z), ten)

    def remote(n, src, dst, to):
        return pltpu.make_async_remote_copy(
            src_ref=src, dst_ref=dst, send_sem=send_sem.at[n], recv_sem=recv_sem.at[n],
            device_id=to, device_id_type=MESH,
        )

    def send(n, src, dst, to):
        remote(n, src, dst, to).start()

    def arrived(n, dst):
        remote(n, dst, dst, peer("P")).wait_recv()

    def sent(n, src):
        remote(n, src, src, peer("P")).wait_send()

    def plane_send(base, src, dst):
        def one(k, carry):
            send(base + k - 1, src(*plane(k)), dst(k - 1), peer("plane", k))
            return carry

        lax.fori_loop(1, PEERS + 1, one, 0)

    def plane_arrived(base, dst):
        def one(k, carry):
            arrived(base + k - 1, dst(k - 1, *plane(k, -1)))
            return carry

        lax.fori_loop(1, PEERS + 1, one, 0)

    def plane_sent(base, src):
        def one(k, carry):
            sent(base + k - 1, src(*plane(k)))
            return carry

        lax.fori_loop(1, PEERS + 1, one, 0)

    def at(start, size):
        return pl.ds(pl.multiple_of(start, size), size)

    stores = [
        pltpu.make_async_copy(src, dst, store_sem.at[n])
        for n, (src, dst) in enumerate(
            ((merged, merged_out), (grad_stage, grad_out), (ortho_nat, ortho_out), (weight_far, weight_out))
        )
    ]
    loads = [
        pltpu.make_async_copy(src, dst, load_sem.at[n])
        for n, (src, dst) in enumerate(
            ((right_in, right), (grad_in, grad), (act_in, act), (error_in, error), (weight_in, weight))
        )
    ]
    for load in loads:
        load.start()

    partners = [peer(name) for name in ("S", "I", "X", "P")]
    partners += [peer("plane", k) for k in range(1, PEERS + 1)]
    barrier = pltpu.get_barrier_semaphore()
    for to in partners:
        pl.semaphore_signal(barrier, inc=1, device_id=to, device_id_type=MESH)
    pl.semaphore_wait(barrier, len(partners))

    def act_chunk(n):
        return pl.ds(n * WIDE, WIDE)

    def send_act(n):
        send(ACT + n, act_in.at[:, act_chunk(n)], act_far.at[:, act_chunk(n)], peer("P"))

    k_rows = at(core * 2048 + y * 512 + z * 128, 128)
    send(KX, weight_in.at[k_rows, :], weight_far.at[k_rows, :], peer("P"))
    send_act(0)

    own, far = at(ten * TOK, TOK), at(other * TOK, TOK)
    loads[0].wait()
    loads[1].wait()
    right_st[...] = stacked(right[...])
    y_own[...] = folded(dot(right_st[...], grad[far, :], NT))
    send(YSEND, y_own, y_far, peer("P"))
    for n in range(1, EARLY):
        send_act(n)
    y_st[...] = stacked(folded(dot(right_st[...], grad[own, :], NT)))

    loads[2].wait()
    loads[3].wait()

    def left_own(c, carry):
        cols = at(c * 512, 512)
        part = dot(y_st[...], act[:, cols]) + dot(right_st[...], error[cols, :], NT)
        left_part[:RANK, cols] = folded(part)
        return carry

    lax.fori_loop(0, 8, left_own, 0)
    arrived(YSEND, y_far)
    y_st[...] = stacked(y_far[...])

    def left_other(c, carry):
        cols = at(c * 512, 512)
        left_part[RANK:, cols] = folded(dot(y_st[...], act[:, cols]))
        return carry

    lax.fori_loop(0, 8, left_other, 0)

    my_half, sib_half = at(core * 2048, 2048), at((1 - core) * 2048, 2048)
    send(LS, left_part.at[:, sib_half], sib_in, peer("S"))
    arrived(LS, sib_in)

    def add_sibling(c, carry):
        cols = at(c * 512, 512)
        left_half[:, cols] = left_part[:, at(core * 2048 + c * 512, 512)] + sib_in[:, cols]
        return carry

    lax.fori_loop(0, 4, add_sibling, 0)
    def plane_cols(py, pz):
        return at(py * 512 + pz * 128, 128)

    plane_send(LZ, lambda py, pz: left_half.at[:, plane_cols(py, pz)], lambda n: plane_in.at[n])

    def merge_own(n, carry):
        cols = at(n * WIDE, WIDE)
        merged[cols, :] = error[cols, :].astype(F32) + dot(act[:, cols], grad[own, :], TN)
        return carry

    lax.fori_loop(0, 12, merge_own, 0)
    plane_arrived(LZ, lambda n, py, pz: plane_in.at[n])

    def add_plane(n, total):
        return total + plane_in[n]

    left_z[...] = lax.fori_loop(0, PEERS, add_plane, left_half[:, plane_cols(y, z)])
    send(LX, left_z.at[:RANK], x_in.at[0], peer("I"))
    send(LX + 1, left_z.at[RANK:], x_in.at[1], peer("X"))
    send(LX + 2, left_z.at[RANK:], x_in.at[2], peer("P"))
    for n in range(EARLY, PIECES):
        send_act(n)
    half_tok = TOK // 2

    def kg_rows(n):
        return pl.ds(n * half_tok, half_tok)

    def kg_source(n):
        return grad_in.at[at(other * TOK + n * half_tok, half_tok), :]

    def send_kg(n):
        send(KG + n, kg_source(n), grad_far.at[kg_rows(n), :], peer("P"))

    send_kg(0)

    lax.fori_loop(12, 16, merge_own, 0)
    loads[4].wait()

    def input_own(c, carry):
        cols = at(c * 512, 512)
        grad_stage[:, cols] = dot(grad[own, :], weight[cols, :], NT).astype(BF16)
        return carry

    lax.fori_loop(0, 8, input_own, 0)
    stores[1].start()

    for k in range(3):
        arrived(LX + k, x_in.at[k])
    def left_cols(py, pz):
        return at(core * 2048 + py * 512 + pz * 128, 128)

    col_z = left_cols(y, z)
    left[:, col_z] = left_z[:RANK, :] + x_in[0] + x_in[1] + x_in[2]
    plane_send(GZ, lambda py, pz: left.at[:, col_z], lambda n: left.at[:, col_z])
    plane_arrived(GZ, lambda n, py, pz: left.at[:, left_cols(py, pz)])
    send(GS, left.at[:, my_half], left.at[:, my_half], peer("S"))
    arrived(KX, weight_far.at[k_rows, :])
    plane_send(KZ, lambda py, pz: weight_far.at[k_rows, :], lambda n: weight_far.at[k_rows, :])
    arrived(GS, left.at[:, sib_half])

    def gram_step(c, total):
        part = left[:, at(c * 512, 512)]
        return total + dot(part, part, NT, HIGHEST)

    aug[:, :RANK] = lax.fori_loop(0, 8, gram_step, jnp.zeros((RANK, RANK), F32))
    sub = lax.broadcasted_iota(jnp.int32, (RANK, 2 * RANK), 0)
    lane = lax.broadcasted_iota(jnp.int32, (RANK, 2 * RANK), 1)
    aug[:, RANK:] = (sub == lane).astype(F32)[:, :RANK]

    def eliminate(j, carry):
        mat, pivots = carry
        row = jnp.sum(jnp.where(sub == j, mat, 0.0), axis=0, keepdims=True)
        col = jnp.sum(jnp.where(lane == j, mat, 0.0), axis=1, keepdims=True)
        pivot = jnp.sum(jnp.where(lane[:1] == j, row, 0.0), axis=1, keepdims=True)
        pivots = jnp.where(sub == j, pivot, pivots)
        factor = jnp.where(sub > j, col / pivot, 0.0)
        return mat - factor * row, pivots

    mat, pivots = lax.fori_loop(0, RANK, eliminate, (aug[...], jnp.ones((RANK, 2 * RANK), F32)))
    aug[...] = mat / jnp.sqrt(pivots)
    low_inv[...] = aug[:, RANK:]

    def ortho_step(c, carry):
        cols = at(c * 512, 512)
        high, low = halves(dot(low_inv[...], left[:, cols], precision=HIGHEST))
        ortho_st[:RANK, cols] = high
        ortho_st[RANK:, cols] = low
        ortho_nat[cols, :] = jnp.concatenate((high, low), axis=0).T
        return carry

    lax.fori_loop(0, 8, ortho_step, 0)
    stores[2].start()

    acc[...] = jnp.zeros_like(acc)
    acc_far[...] = jnp.zeros_like(acc_far)

    def right_own(c, carry):
        cols = at(c * 512, 512)
        acc[...] += dot(ortho_st[:, cols], act[:, cols], NT)
        return carry

    lax.fori_loop(0, 8, right_own, 0)
    y_st[...] = stacked(folded(acc[...]))
    acc[...] = dot(y_st[...], grad[own, :])

    def right_error(c, carry):
        cols = at(c * 512, 512)
        acc[...] += dot(ortho_st[:, cols], error[cols, :])
        return carry

    lax.fori_loop(0, 8, right_error, 0)

    def merge_far(n, carry):
        cols = at(n * WIDE, WIDE)
        arrived(ACT + n, act_far.at[:, cols])
        piece = act_far[:, cols]
        merged[cols, :] += dot(piece, grad[far, :], TN)
        pltpu.make_async_copy(merged.at[cols, :], merged_out.at[cols, :], store_sem.at[0]).start()
        acc_far[...] += dot(ortho_st[:, cols], piece, NT)
        return carry

    lax.fori_loop(0, 12, merge_far, 0)
    plane_arrived(KZ, lambda n, py, pz: weight_far.at[left_cols(py, pz), :])
    send(KS, weight_far.at[my_half, :], weight_far.at[my_half, :], peer("S"))
    early = {
        YSEND: y_own, KX: weight_in.at[k_rows, :], LS: left_part.at[:, sib_half], LX: left_z.at[:RANK],
        LX + 1: left_z.at[RANK:], LX + 2: left_z.at[RANK:], GS: left.at[:, my_half],
    }
    for n, src in early.items():
        sent(n, src)
    plane_sent(KZ, lambda py, pz: weight_far.at[k_rows, :])
    plane_sent(LZ, lambda py, pz: left_half.at[:, plane_cols(py, pz)])
    plane_sent(GZ, lambda py, pz: left.at[:, col_z])
    lax.fori_loop(12, PIECES, merge_far, 0)
    y_st[...] = stacked(folded(acc_far[...]))
    r0[...] = folded(acc[...] + dot(y_st[...], grad[far, :]))

    r_mine, r_other = at(core * 256, 256), at((1 - core) * 256, 256)
    send(RS, r0.at[:, r_other], r_sib, peer("S"))
    arrived(KS, weight_far.at[sib_half, :])
    stores[3].start()
    arrived(RS, r_sib)
    r1[...] = r0[:, r_mine] + r_sib[...]

    def right_block(py, pz):
        return at(py * 16 + lax.div(pz, 2) * 8, 8), at(lax.rem(pz, 2) * 128, 128)

    plane_send(RZ, lambda py, pz: r1.at[right_block(py, pz)], lambda n: r_in.at[n])
    plane_arrived(RZ, lambda n, py, pz: r_in.at[n])

    def add_right(n, total):
        return total + r_in[n]

    r3[...] = lax.fori_loop(0, PEERS, add_right, r1[right_block(y, z)])
    send(RI, r3, r_i, peer("I"))
    send_kg(1)
    for n in range(PIECES):
        sent(ACT + n, act_in.at[:, act_chunk(n)])
    sent(KG, kg_source(0))
    sent(KS, weight_far.at[my_half, :])
    sent(RS, r0.at[:, r_other])
    plane_sent(RZ, lambda py, pz: r1.at[right_block(py, pz)])

    arrived(RI, r_i)

    def full_block(py, pz):
        return (
            at(py * 16 + lax.div(pz, 2) * 8, 8),
            at(core * 256 + lax.rem(pz, 2) * 128, 128),
        )

    mine = full_block(y, z)
    right_full[mine] = (r3[...] + r_i[...]) * (1.0 / 64.0)
    plane_send(BZ, lambda py, pz: right_full.at[mine], lambda n: right_full.at[mine])
    plane_arrived(BZ, lambda n, py, pz: right_full.at[full_block(py, pz)])
    send(BS, right_full.at[:, r_mine], right_full.at[:, r_mine], peer("S"))
    arrived(BS, right_full.at[:, r_other])
    right_out[...] = right_full[...]
    for n in range(2):
        arrived(KG + n, grad_far.at[kg_rows(n), :])
    for store in stores:
        store.wait()

    late = {KG + 1: kg_source(1), RI: r3, BS: right_full.at[:, r_mine]}
    for n, src in late.items():
        sent(n, src)
    plane_sent(BZ, lambda py, pz: right_full.at[mine])


def finish(merged, ortho, right, grad_own, weight_far, grad_far, input_grad, right_new, error_new):
    high, low = halves(right[...])
    approx = dot(ortho[...], jnp.concatenate((high, high), axis=0)) + dot(ortho[:, :RANK], low)
    error_new[...] = (merged[...] - approx).astype(BF16)
    term = dot(grad_far[...], weight_far[...], NT).astype(BF16)
    input_grad[...] = (grad_own[...].astype(F32) + term.astype(F32)).astype(BF16)
    right_new[...] = right[...]


def shards(activations, key_grad, key_weight, error_prev, right_prev):
    def vmem(*shape, kind=F32):
        return pltpu.VMEM(shape, kind)

    def array(*shape, kind=BF16):
        return jax.ShapeDtypeStruct(shape, kind)

    anywhere = pl.BlockSpec(memory_space=pl.ANY)
    right, merged, ortho, grad_own, grad_far, weight_far = pl.pallas_call(
        kernel,
        out_shape=(
            array(RANK, COLS, kind=F32),
            array(D, COLS, kind=F32),
            array(D, 2 * RANK),
            array(TOK, D),
            array(TOK, COLS),
            array(D, COLS),
        ),
        in_specs=[anywhere] * 5,
        out_specs=(pl.BlockSpec(memory_space=pltpu.VMEM),) + (anywhere,) * 5,
        scratch_shapes=[
            vmem(TOK, D, kind=BF16),
            vmem(TOK, D, kind=BF16),
            vmem(D, COLS, kind=BF16),
            vmem(2 * TOK, COLS, kind=BF16),
            vmem(D, COLS, kind=BF16),
            vmem(D, COLS, kind=BF16),
            vmem(RANK, COLS),
            vmem(2 * RANK, COLS, kind=BF16),
            vmem(2 * RANK, TOK, kind=BF16),
            vmem(RANK, TOK),
            vmem(RANK, TOK),
            vmem(2 * RANK, D),
            vmem(2 * RANK, D // 2),
            vmem(2 * RANK, D // 2),
            vmem(PEERS, 2 * RANK, 128),
            vmem(2 * RANK, 128),
            vmem(3, RANK, 128),
            vmem(RANK, D),
            vmem(RANK, 2 * RANK),
            vmem(RANK, RANK),
            vmem(2 * RANK, D, kind=BF16),
            vmem(D, 2 * RANK, kind=BF16),
            vmem(D, COLS),
            vmem(TOK, D, kind=BF16),
            vmem(2 * RANK, COLS),
            vmem(2 * RANK, TOK),
            vmem(RANK, COLS),
            vmem(RANK, 256),
            vmem(RANK, 256),
            vmem(PEERS, 8, 128),
            vmem(8, 128),
            vmem(8, 128),
            vmem(RANK, COLS),
            pltpu.SemaphoreType.DMA((5,)),
            pltpu.SemaphoreType.DMA((4,)),
            pltpu.SemaphoreType.DMA((N_COPIES,)),
            pltpu.SemaphoreType.DMA((N_COPIES,)),
        ],
        compiler_params=pltpu.CompilerParams(
            collective_id=0, has_side_effects=True, vmem_limit_bytes=60 * 2**20
        ),
    )(activations, key_grad, key_weight, error_prev, right_prev.T)
    steps = 4
    rows, cols = D // steps, D // steps

    def whole(*shape):
        return pl.BlockSpec(shape, lambda i: (0, 0))

    def down(*shape):
        return pl.BlockSpec(shape, lambda i: (i, 0))

    def along(*shape):
        return pl.BlockSpec(shape, lambda i: (0, i))

    input_grad, right_new, error_new = pl.pallas_call(
        finish,
        grid=(steps,),
        out_shape=(array(TOK, D), array(RANK, COLS, kind=F32), array(D, COLS)),
        in_specs=[
            down(rows, COLS), down(rows, 2 * RANK), whole(RANK, COLS),
            along(TOK, cols), down(cols, COLS), whole(TOK, COLS),
        ],
        out_specs=(along(TOK, cols), whole(RANK, COLS), down(rows, COLS)),
        compiler_params=pltpu.CompilerParams(vmem_limit_bytes=60 * 2**20),
    )(merged, ortho, right, grad_own, weight_far, grad_far)
    return input_grad, right_new.T, error_new


def solution(mesh):
    placed = (
        P(("dp", "tensor"), None),
        P("dp", "tensor"),
        P(None, "tensor"),
        P("dp", "tensor"),
        P("tensor", None),
    )
    return jax.shard_map(
        shards,
        mesh=mesh,
        in_specs=placed,
        out_specs=(P(("dp", "tensor"), None), P("tensor", None), P("dp", "tensor")),
        check_vma=False,
    )
```

```python
import jax
import jax.numpy as jnp
from jax import lax
from jax.experimental import pallas as pl
from jax.experimental.pallas import tpu as pltpu
from jax.sharding import PartitionSpec as P

MESH = pl.DeviceIdType.MESH
HIGHEST = lax.Precision.HIGHEST
F32, BF16 = jnp.float32, jnp.bfloat16

TOK = 512
D = 4096
COLS = 512
RANK = 64
PIECES = 16
WIDE = D // PIECES
EARLY = 6

PEERS = 15
ACT = 0
YSEND = ACT + PIECES
KX, KZ, KS = YSEND + 1, YSEND + 2, YSEND + 2 + PEERS
LS, LZ, LX = KS + 1, KS + 2, KS + 2 + PEERS
GZ, GS = LX + 3, LX + 3 + PEERS
KG = GS + 1
RS, RZ, RI = KG + 2, KG + 3, KG + 3 + PEERS
BZ, BS = RI + 1, RI + 1 + PEERS
N_COPIES = BS + 1


def halves(value):
    high = value.astype(BF16)
    return high, (value - high.astype(F32)).astype(BF16)


def stacked(value):
    return jnp.concatenate(halves(value), axis=0)


def folded(value):
    half = value.shape[0] // 2
    return value[:half] + value[half:]


def dot(a, b, dims=((1,), (0,)), precision=None):
    return lax.dot_general(a, b, (dims, ((), ())), precision=precision, preferred_element_type=F32)


NT = ((1,), (1,))
TN = ((0,), (0,))


def kernel(
    act_in, grad_in, weight_in, error_in, right_in,
    right_out, merged_out, ortho_out, grad_out, grad_far, weight_out,
    act, act_far, error, grad, weight, weight_far, right,
    right_st, y_st, y_own, y_far, left_part, sib_in, left_half, plane_in, left_z, x_in,
    left, aug, low_inv, ortho_st, ortho_nat, merged, grad_stage, acc, acc_far,
    r0, r_sib, r1, r_in, r3, r_i, right_full,
    load_sem, store_sem, send_sem, recv_sem,
):
    dp, ten = lax.axis_index("dp"), lax.axis_index("tensor")
    z, y = lax.div(dp, 16), lax.rem(lax.div(dp, 4), 4)
    x_lo, core = lax.rem(lax.div(dp, 2), 2), lax.rem(dp, 2)
    other = 1 - ten

    def plane(k, sign=1):
        return lax.rem(y + sign * lax.div(k, 4) + 4, 4), lax.rem(z + sign * lax.rem(k, 4) + 4, 4)

    def peer(name, k=0):
        flipped = dp + 2 - 4 * x_lo
        if name == "S":
            return (dp + 1 - 2 * core, ten)
        if name == "I":
            return (flipped, ten)
        if name == "X":
            return (flipped, other)
        if name == "P":
            return (dp, other)
        py, pz = plane(k)
        return (dp + 4 * (py - y) + 16 * (pz - z), ten)

    def remote(n, src, dst, to):
        return pltpu.make_async_remote_copy(
            src_ref=src, dst_ref=dst, send_sem=send_sem.at[n], recv_sem=recv_sem.at[n],
            device_id=to, device_id_type=MESH,
        )

    def send(n, src, dst, to):
        remote(n, src, dst, to).start()

    def arrived(n, dst):
        remote(n, dst, dst, peer("P")).wait_recv()

    def sent(n, src):
        remote(n, src, src, peer("P")).wait_send()

    def plane_send(base, src, dst):
        def one(k, carry):
            send(base + k - 1, src(*plane(k)), dst(k - 1), peer("plane", k))
            return carry

        lax.fori_loop(1, PEERS + 1, one, 0)

    def plane_arrived(base, dst):
        def one(k, carry):
            arrived(base + k - 1, dst(k - 1, *plane(k, -1)))
            return carry

        lax.fori_loop(1, PEERS + 1, one, 0)

    def plane_sent(base, src):
        def one(k, carry):
            sent(base + k - 1, src(*plane(k)))
            return carry

        lax.fori_loop(1, PEERS + 1, one, 0)

    def at(start, size):
        return pl.ds(pl.multiple_of(start, size), size)

    stores = [
        pltpu.make_async_copy(src, dst, store_sem.at[n])
        for n, (src, dst) in enumerate(
            ((merged, merged_out), (grad_stage, grad_out), (ortho_nat, ortho_out), (weight_far, weight_out))
        )
    ]
    loads = [
        pltpu.make_async_copy(src, dst, load_sem.at[n])
        for n, (src, dst) in enumerate(
            ((right_in, right), (grad_in, grad), (act_in, act), (error_in, error), (weight_in, weight))
        )
    ]
    for load in loads:
        load.start()

    partners = [peer(name) for name in ("S", "I", "X", "P")]
    partners += [peer("plane", k) for k in range(1, PEERS + 1)]
    barrier = pltpu.get_barrier_semaphore()
    for to in partners:
        pl.semaphore_signal(barrier, inc=1, device_id=to, device_id_type=MESH)
    pl.semaphore_wait(barrier, len(partners))

    def act_chunk(n):
        return pl.ds(n * WIDE, WIDE)

    def send_act(n):
        send(ACT + n, act_in.at[:, act_chunk(n)], act_far.at[:, act_chunk(n)], peer("P"))

    k_rows = at(core * 2048 + y * 512 + z * 128, 128)
    send(KX, weight_in.at[k_rows, :], weight_far.at[k_rows, :], peer("P"))
    send_act(0)

    own, far = at(ten * TOK, TOK), at(other * TOK, TOK)
    loads[0].wait()
    loads[1].wait()
    right_st[...] = stacked(right[...])
    y_own[...] = folded(dot(right_st[...], grad[far, :], NT))
    send(YSEND, y_own, y_far, peer("P"))
    for n in range(1, EARLY):
        send_act(n)
    y_st[...] = stacked(folded(dot(right_st[...], grad[own, :], NT)))

    loads[2].wait()
    loads[3].wait()

    def left_own(c, carry):
        cols = at(c * 512, 512)
        part = dot(y_st[...], act[:, cols]) + dot(right_st[...], error[cols, :], NT)
        left_part[:RANK, cols] = folded(part)
        return carry

    lax.fori_loop(0, 8, left_own, 0)
    arrived(YSEND, y_far)
    y_st[...] = stacked(y_far[...])

    def left_other(c, carry):
        cols = at(c * 512, 512)
        left_part[RANK:, cols] = folded(dot(y_st[...], act[:, cols]))
        return carry

    lax.fori_loop(0, 8, left_other, 0)

    my_half, sib_half = at(core * 2048, 2048), at((1 - core) * 2048, 2048)
    send(LS, left_part.at[:, sib_half], sib_in, peer("S"))
    arrived(LS, sib_in)

    def add_sibling(c, carry):
        cols = at(c * 512, 512)
        left_half[:, cols] = left_part[:, at(core * 2048 + c * 512, 512)] + sib_in[:, cols]
        return carry

    lax.fori_loop(0, 4, add_sibling, 0)
    def plane_cols(py, pz):
        return at(py * 512 + pz * 128, 128)

    plane_send(LZ, lambda py, pz: left_half.at[:, plane_cols(py, pz)], lambda n: plane_in.at[n])

    def merge_own(n, carry):
        cols = at(n * WIDE, WIDE)
        merged[cols, :] = error[cols, :].astype(F32) + dot(act[:, cols], grad[own, :], TN)
        return carry

    lax.fori_loop(0, 12, merge_own, 0)
    plane_arrived(LZ, lambda n, py, pz: plane_in.at[n])

    def add_plane(n, total):
        return total + plane_in[n]

    left_z[...] = lax.fori_loop(0, PEERS, add_plane, left_half[:, plane_cols(y, z)])
    send(LX, left_z.at[:RANK], x_in.at[0], peer("I"))
    send(LX + 1, left_z.at[RANK:], x_in.at[1], peer("X"))
    send(LX + 2, left_z.at[RANK:], x_in.at[2], peer("P"))
    for n in range(EARLY, PIECES):
        send_act(n)
    half_tok = TOK // 2

    def kg_rows(n):
        return pl.ds(n * half_tok, half_tok)

    def kg_source(n):
        return grad_in.at[at(other * TOK + n * half_tok, half_tok), :]

    def send_kg(n):
        send(KG + n, kg_source(n), grad_far.at[kg_rows(n), :], peer("P"))

    send_kg(0)

    lax.fori_loop(12, 16, merge_own, 0)
    loads[4].wait()

    def input_own(c, carry):
        cols = at(c * 512, 512)
        grad_stage[:, cols] = dot(grad[own, :], weight[cols, :], NT).astype(BF16)
        return carry

    lax.fori_loop(0, 8, input_own, 0)
    stores[1].start()

    for k in range(3):
        arrived(LX + k, x_in.at[k])
    def left_cols(py, pz):
        return at(core * 2048 + py * 512 + pz * 128, 128)

    col_z = left_cols(y, z)
    left[:, col_z] = left_z[:RANK, :] + x_in[0] + x_in[1] + x_in[2]
    plane_send(GZ, lambda py, pz: left.at[:, col_z], lambda n: left.at[:, col_z])
    plane_arrived(GZ, lambda n, py, pz: left.at[:, left_cols(py, pz)])
    send(GS, left.at[:, my_half], left.at[:, my_half], peer("S"))
    arrived(KX, weight_far.at[k_rows, :])
    plane_send(KZ, lambda py, pz: weight_far.at[k_rows, :], lambda n: weight_far.at[k_rows, :])
    arrived(GS, left.at[:, sib_half])

    def gram_step(c, total):
        part = left[:, at(c * 512, 512)]
        return total + dot(part, part, NT, HIGHEST)

    aug[:, :RANK] = lax.fori_loop(0, 8, gram_step, jnp.zeros((RANK, RANK), F32))
    sub = lax.broadcasted_iota(jnp.int32, (RANK, 2 * RANK), 0)
    lane = lax.broadcasted_iota(jnp.int32, (RANK, 2 * RANK), 1)
    aug[:, RANK:] = (sub == lane).astype(F32)[:, :RANK]

    def eliminate(j, carry):
        mat, pivots = carry
        row = jnp.sum(jnp.where(sub == j, mat, 0.0), axis=0, keepdims=True)
        col = jnp.sum(jnp.where(lane == j, mat, 0.0), axis=1, keepdims=True)
        pivot = jnp.sum(jnp.where(lane[:1] == j, row, 0.0), axis=1, keepdims=True)
        pivots = jnp.where(sub == j, pivot, pivots)
        factor = jnp.where(sub > j, col / pivot, 0.0)
        return mat - factor * row, pivots

    mat, pivots = lax.fori_loop(0, RANK, eliminate, (aug[...], jnp.ones((RANK, 2 * RANK), F32)))
    aug[...] = mat / jnp.sqrt(pivots)
    low_inv[...] = aug[:, RANK:]

    def ortho_step(c, carry):
        cols = at(c * 512, 512)
        high, low = halves(dot(low_inv[...], left[:, cols], precision=HIGHEST))
        ortho_st[:RANK, cols] = high
        ortho_st[RANK:, cols] = low
        ortho_nat[cols, :] = jnp.concatenate((high, low), axis=0).T
        return carry

    lax.fori_loop(0, 8, ortho_step, 0)
    stores[2].start()

    acc[...] = jnp.zeros_like(acc)
    acc_far[...] = jnp.zeros_like(acc_far)

    def right_own(c, carry):
        cols = at(c * 512, 512)
        acc[...] += dot(ortho_st[:, cols], act[:, cols], NT)
        return carry

    lax.fori_loop(0, 8, right_own, 0)
    y_st[...] = stacked(folded(acc[...]))
    acc[...] = dot(y_st[...], grad[own, :])

    def right_error(c, carry):
        cols = at(c * 512, 512)
        acc[...] += dot(ortho_st[:, cols], error[cols, :])
        return carry

    lax.fori_loop(0, 8, right_error, 0)

    def merge_far(n, carry):
        cols = at(n * WIDE, WIDE)
        arrived(ACT + n, act_far.at[:, cols])
        piece = act_far[:, cols]
        merged[cols, :] += dot(piece, grad[far, :], TN)
        pltpu.make_async_copy(merged.at[cols, :], merged_out.at[cols, :], store_sem.at[0]).start()
        acc_far[...] += dot(ortho_st[:, cols], piece, NT)
        return carry

    lax.fori_loop(0, 12, merge_far, 0)
    plane_arrived(KZ, lambda n, py, pz: weight_far.at[left_cols(py, pz), :])
    send(KS, weight_far.at[my_half, :], weight_far.at[my_half, :], peer("S"))
    early = {
        YSEND: y_own, KX: weight_in.at[k_rows, :], LS: left_part.at[:, sib_half], LX: left_z.at[:RANK],
        LX + 1: left_z.at[RANK:], LX + 2: left_z.at[RANK:], GS: left.at[:, my_half],
    }
    for n, src in early.items():
        sent(n, src)
    plane_sent(KZ, lambda py, pz: weight_far.at[k_rows, :])
    plane_sent(LZ, lambda py, pz: left_half.at[:, plane_cols(py, pz)])
    plane_sent(GZ, lambda py, pz: left.at[:, col_z])
    lax.fori_loop(12, PIECES, merge_far, 0)
    y_st[...] = stacked(folded(acc_far[...]))
    r0[...] = folded(acc[...] + dot(y_st[...], grad[far, :]))

    r_mine, r_other = at(core * 256, 256), at((1 - core) * 256, 256)
    send(RS, r0.at[:, r_other], r_sib, peer("S"))
    arrived(KS, weight_far.at[sib_half, :])
    stores[3].start()
    arrived(RS, r_sib)
    r1[...] = r0[:, r_mine] + r_sib[...]

    def right_block(py, pz):
        return at(py * 16 + lax.div(pz, 2) * 8, 8), at(lax.rem(pz, 2) * 128, 128)

    plane_send(RZ, lambda py, pz: r1.at[right_block(py, pz)], lambda n: r_in.at[n])
    plane_arrived(RZ, lambda n, py, pz: r_in.at[n])

    def add_right(n, total):
        return total + r_in[n]

    r3[...] = lax.fori_loop(0, PEERS, add_right, r1[right_block(y, z)])
    send(RI, r3, r_i, peer("I"))
    send_kg(1)
    for n in range(PIECES):
        sent(ACT + n, act_in.at[:, act_chunk(n)])
    sent(KG, kg_source(0))
    sent(KS, weight_far.at[my_half, :])
    sent(RS, r0.at[:, r_other])
    plane_sent(RZ, lambda py, pz: r1.at[right_block(py, pz)])

    arrived(RI, r_i)

    def full_block(py, pz):
        return (
            at(py * 16 + lax.div(pz, 2) * 8, 8),
            at(core * 256 + lax.rem(pz, 2) * 128, 128),
        )

    mine = full_block(y, z)
    right_full[mine] = (r3[...] + r_i[...]) * (1.0 / 64.0)
    plane_send(BZ, lambda py, pz: right_full.at[mine], lambda n: right_full.at[mine])
    plane_arrived(BZ, lambda n, py, pz: right_full.at[full_block(py, pz)])
    send(BS, right_full.at[:, r_mine], right_full.at[:, r_mine], peer("S"))
    arrived(BS, right_full.at[:, r_other])
    right_out[...] = right_full[...]
    for n in range(2):
        arrived(KG + n, grad_far.at[kg_rows(n), :])
    for store in stores:
        store.wait()

    late = {KG + 1: kg_source(1), RI: r3, BS: right_full.at[:, r_mine]}
    for n, src in late.items():
        sent(n, src)
    plane_sent(BZ, lambda py, pz: right_full.at[mine])


def finish(merged, ortho, right, grad_own, weight_far, grad_far, input_grad, right_new, error_new):
    high, low = halves(right[...])
    approx = dot(ortho[...], jnp.concatenate((high, high), axis=0)) + dot(ortho[:, :RANK], low)
    error_new[...] = (merged[...] - approx).astype(BF16)
    term = dot(grad_far[...], weight_far[...], NT).astype(BF16)
    input_grad[...] = (grad_own[...].astype(F32) + term.astype(F32)).astype(BF16)
    right_new[...] = right[...]


def shards(activations, key_grad, key_weight, error_prev, right_prev):
    def vmem(*shape, kind=F32):
        return pltpu.VMEM(shape, kind)

    def array(*shape, kind=BF16):
        return jax.ShapeDtypeStruct(shape, kind)

    anywhere = pl.BlockSpec(memory_space=pl.ANY)
    right, merged, ortho, grad_own, grad_far, weight_far = pl.pallas_call(
        kernel,
        out_shape=(
            array(RANK, COLS, kind=F32),
            array(D, COLS, kind=F32),
            array(D, 2 * RANK),
            array(TOK, D),
            array(TOK, COLS),
            array(D, COLS),
        ),
        in_specs=[anywhere] * 5,
        out_specs=(pl.BlockSpec(memory_space=pltpu.VMEM),) + (anywhere,) * 5,
        scratch_shapes=[
            vmem(TOK, D, kind=BF16),
            vmem(TOK, D, kind=BF16),
            vmem(D, COLS, kind=BF16),
            vmem(2 * TOK, COLS, kind=BF16),
            vmem(D, COLS, kind=BF16),
            vmem(D, COLS, kind=BF16),
            vmem(RANK, COLS),
            vmem(2 * RANK, COLS, kind=BF16),
            vmem(2 * RANK, TOK, kind=BF16),
            vmem(RANK, TOK),
            vmem(RANK, TOK),
            vmem(2 * RANK, D),
            vmem(2 * RANK, D // 2),
            vmem(2 * RANK, D // 2),
            vmem(PEERS, 2 * RANK, 128),
            vmem(2 * RANK, 128),
            vmem(3, RANK, 128),
            vmem(RANK, D),
            vmem(RANK, 2 * RANK),
            vmem(RANK, RANK),
            vmem(2 * RANK, D, kind=BF16),
            vmem(D, 2 * RANK, kind=BF16),
            vmem(D, COLS),
            vmem(TOK, D, kind=BF16),
            vmem(2 * RANK, COLS),
            vmem(2 * RANK, TOK),
            vmem(RANK, COLS),
            vmem(RANK, 256),
            vmem(RANK, 256),
            vmem(PEERS, 8, 128),
            vmem(8, 128),
            vmem(8, 128),
            vmem(RANK, COLS),
            pltpu.SemaphoreType.DMA((5,)),
            pltpu.SemaphoreType.DMA((4,)),
            pltpu.SemaphoreType.DMA((N_COPIES,)),
            pltpu.SemaphoreType.DMA((N_COPIES,)),
        ],
        compiler_params=pltpu.CompilerParams(
            collective_id=0, has_side_effects=True, vmem_limit_bytes=46 * 2**20
        ),
    )(activations, key_grad, key_weight, error_prev, right_prev.T)
    steps = 4
    rows, cols = D // steps, D // steps

    def whole(*shape):
        return pl.BlockSpec(shape, lambda i: (0, 0))

    def down(*shape):
        return pl.BlockSpec(shape, lambda i: (i, 0))

    def along(*shape):
        return pl.BlockSpec(shape, lambda i: (0, i))

    input_grad, right_new, error_new = pl.pallas_call(
        finish,
        grid=(steps,),
        out_shape=(array(TOK, D), array(RANK, COLS, kind=F32), array(D, COLS)),
        in_specs=[
            down(rows, COLS), down(rows, 2 * RANK), whole(RANK, COLS),
            along(TOK, cols), down(cols, COLS), whole(TOK, COLS),
        ],
        out_specs=(along(TOK, cols), whole(RANK, COLS), down(rows, COLS)),
        compiler_params=pltpu.CompilerParams(vmem_limit_bytes=47 * 2**20),
    )(merged, ortho, right, grad_own, weight_far, grad_far)
    return input_grad, right_new.T, error_new


def solution(mesh):
    placed = (
        P(("dp", "tensor"), None),
        P("dp", "tensor"),
        P(None, "tensor"),
        P("dp", "tensor"),
        P("tensor", None),
    )
    return jax.shard_map(
        shards,
        mesh=mesh,
        in_specs=placed,
        out_specs=(P(("dp", "tensor"), None), P("tensor", None), P("dp", "tensor")),
        check_vma=False,
    )
```
